512 devices in a mesh: grp: 16 (over z, core), seq: 32 (over y, x).
Axes of the slice: x: 4, y: 8, z: 8, core: 2. Of those that a mesh axis runs over, the one named last changes fastest.
Arguments:
- hist_keys: bfloat16 [16, 4096, 1024], P('grp', 'seq'), may hold values from -4 to 4
- hist_values: bfloat16 [16, 4096, 1024], P('grp', 'seq'), may hold values from -6 to 6
- latent_queries: bfloat16 [16, 64, 1024], P('grp', 'seq'), may hold values from -48 to 48
- latent_pos: int32 [16, 64], P('grp'), may hold values from 512 to 4095
- targets: int32 [16, 64], P('grp', 'seq'), may hold values from 0 to 127
- out_proj: bfloat16 [1024, 2048], P('seq'), may hold values from -0.1875 to 0.1875
- norm_gain: float32 [2048], replicated, may hold values from 0.1 to 1.9
- unembed: bfloat16 [2048, 128], replicated, may hold values from -0.125 to 0.125
Outputs:
- loss: float32 [16], P('grp')
- grad_queries: bfloat16 [16, 64, 1024], P('grp', 'seq')
- grad_keys: bfloat16 [16, 4096, 1024], P('grp', 'seq')
- grad_values: bfloat16 [16, 4096, 1024], P('grp', 'seq')
- proj_update: float32 [1024, 2048], P('seq')
The draws below stay inside these ranges and needn't reach their ends.
All inputs are finite; a program needn't handle non-finite values.
Results may differ from the reference program's by a relative error of at most 0.03.
Values may be sent and summed in bfloat16 or wider, within the bound.
A program may use at most 64 MiB of HBM per device.

```python
import math
import jax
import jax.numpy as jnp
import numpy as np
from jax import lax

D = 2048
HEADS = 8
HD = 128
VOCAB = 128
NL = 64
TOK_DEV = 128
HC = 1024
LENGTH = 4096
SEQS = 16
N_SEQ = 32


def shared_keys(key):
    base = jax.random.fold_in(key, 7)
    first = jax.random.fold_in(base, 0)
    channels = HEADS * HD
    keys_all = jnp.clip(jax.random.normal(first, (SEQS, LENGTH, channels), jnp.float32), -4.0, 4.0)
    return keys_all


def draw_hist_keys(key, part):
    keys_all = shared_keys(key)
    return keys_all.astype(jnp.bfloat16)


def draw_latent_queries(key, part):
    own_key = jax.random.fold_in(key, 11)
    first = jax.random.fold_in(own_key, 0)
    queries = jnp.clip(jax.random.normal(first, (SEQS, NL, HEADS * HD), jnp.float32), -4.0, 4.0)
    return queries.astype(jnp.bfloat16)


def with_ends(values, stream_key, least, top_value):
    longest = values.shape.index(max(values.shape))
    spots = []
    for shift in (0, 1):
        where = [jax.random.randint(jax.random.fold_in(stream_key, axis), (), 0, length) for axis, length in enumerate(values.shape)]
        where[longest] = (where[longest] + shift) % values.shape[longest]
        spots.append(tuple(where))
    return values.at[spots[0]].set(least).at[spots[1]].set(top_value)


def levels(key, dims, pieces, least, top_value):
    def one(dim, shards_of):
        heights = jax.random.uniform(jax.random.fold_in(jax.random.fold_in(key, 6), dim), (shards_of,), jnp.float32, least / len(pieces), top_value / len(pieces))
        return jnp.repeat(jnp.exp(heights), dims[dim] // shards_of).reshape((-1,) + (1,) * (len(dims) - dim - 1))

    loudness = one(*pieces[0])
    for cut in pieces[1:]:
        loudness = loudness * one(*cut)
    return loudness


def cumulative_ranks(count, slope):
    weights = [(1 << 20) // math.isqrt(rank ** slope) + 1 for rank in range(1, count + 1)]
    deviation = 1 + sum(weights) // (1 << 30)
    return np.cumsum(np.array([max(1, weight // deviation) for weight in weights]))


def ranked(key, dims, count, skew):
    listing = cumulative_ranks(count, skew)
    pick = jax.random.randint(jax.random.fold_in(key, 1), dims, 0, int(listing[count - 1]))
    grade = jnp.searchsorted(jnp.asarray(listing, jnp.int32), pick, side="right")
    return jax.random.permutation(jax.random.fold_in(key, 2), count)[grade].astype(jnp.int32)


def bell_draw(key, extent, deviation, limit, cuts=(), held_as=jnp.bfloat16):
    result = jax.random.normal(key, extent, jnp.float32) * deviation
    if len(cuts) > 0:
        result = levels(key, extent, cuts, -0.22, 0.18) * result
    return jnp.clip(result, min=-limit, max=limit).astype(held_as)


def setup_inputs(seed: int = 0) -> dict:
    seeds = jax.random.split(jax.random.key(seed), 9)
    return {
        "hist_keys": draw_hist_keys(jax.random.fold_in(seeds[8], 71), 0),
        "hist_values": bell_draw(seeds[1], (SEQS, LENGTH, HC), 1.0, 6.0, ((0, 16), (1, 32))),
        "latent_queries": draw_latent_queries(jax.random.fold_in(seeds[8], 71), 0),
        "latent_pos": with_ends(jax.random.randint(seeds[3], (SEQS, NL), LENGTH // 8, LENGTH), jax.random.fold_in(seeds[3], 1), LENGTH // 8, LENGTH - 1).astype(jnp.int32),
        "targets": with_ends(ranked(seeds[4], (SEQS, NL), VOCAB, 2), jax.random.fold_in(seeds[4], 3), 0, VOCAB - 1).astype(jnp.int32),
        "out_proj": bell_draw(seeds[5], (HC, D), HC ** -0.5, 0.1875, ((0, 32),)),
        "norm_gain": jnp.clip(1.0 + 0.18 * jax.random.normal(seeds[6], (D,), jnp.float32), 0.1, 1.9),
        "unembed": bell_draw(seeds[7], (D, VOCAB), D ** -0.5, 0.125),
    }


epsilon = 1e-06
loss_factor = 64.0

def head_split(array):
    return array.reshape(array.shape[0], -1, HD)

def reference(hist_keys, hist_values, latent_queries, latent_pos, targets, out_proj, norm_gain, unembed):
    softmax_scale = HD ** (-0.5)
    channels = HEADS * HD
    block_starts = jnp.arange(N_SEQ, dtype=jnp.int32) * TOK_DEV

    def one_sequence(carried, inputs):
        seq_keys, seq_values, seq_queries, positions, seq_targets = inputs
        query_heads = head_split(seq_queries.astype(jnp.float32))
        key_blocks = seq_keys.reshape(N_SEQ, TOK_DEV, channels)
        value_blocks = seq_values.reshape(N_SEQ, TOK_DEV, channels)

        def block_scores(block_keys, block_start):
            scores = jnp.einsum('ihd,jhd->hij', query_heads, head_split(block_keys.astype(jnp.float32))) * softmax_scale
            places = block_start + jnp.arange(TOK_DEV, dtype=jnp.int32)
            visible = (places[None, :] <= positions[:, None])[None]
            return (scores, visible)

        def forward_block(block_inputs):
            block_keys, block_values, block_start = block_inputs
            scores, visible = block_scores(block_keys, block_start)
            largest = lax.optimization_barrier(jnp.max(jnp.where(visible, scores, -1e+30), axis=-1))
            weights = jnp.where(visible, jnp.exp(scores - largest[..., None]), 0.0)
            summed = lax.optimization_barrier(jnp.sum(weights, axis=-1))
            rounded = weights.astype(jnp.bfloat16).astype(jnp.float32)
            partial_out = jnp.einsum('hij,jhd->ihd', rounded, head_split(block_values.astype(jnp.float32)))
            return (largest.T, summed.T, partial_out.reshape(NL, channels))
        maxima, sums, partials = lax.map(forward_block, (key_blocks, value_blocks, block_starts))
        best = lax.optimization_barrier(jnp.max(maxima, axis=0))
        factors = jnp.exp(maxima - best)
        denom = lax.optimization_barrier(jnp.sum(sums * factors, axis=0))
        combined = lax.optimization_barrier(jnp.sum(partials * jnp.repeat(factors, HD, axis=-1), axis=0))
        attn = (combined / jnp.repeat(denom, HD, axis=-1)).astype(jnp.bfloat16)
        log_norm = best + jnp.log(denom)
        hidden = jnp.dot(attn, out_proj, preferred_element_type=jnp.float32)
        inverse = lax.rsqrt(lax.optimization_barrier(jnp.mean(hidden * hidden, axis=-1, keepdims=True)) + epsilon)
        normed = (hidden * inverse * norm_gain).astype(jnp.bfloat16)
        logits = jnp.dot(normed, unembed, preferred_element_type=jnp.float32)
        log_total = jax.nn.logsumexp(logits, axis=-1, keepdims=True)
        onehot = (jnp.arange(VOCAB, dtype=jnp.int32)[None, :] == seq_targets[:, None]).astype(jnp.float32)
        seq_loss = jnp.sum(log_total[:, 0] - lax.optimization_barrier(jnp.sum(logits * onehot, axis=-1)))
        grad_logits = (loss_factor * (jnp.exp(logits - log_total) - onehot)).astype(jnp.bfloat16)
        grad_normed = jnp.dot(grad_logits, unembed.T, preferred_element_type=jnp.float32)
        scaled = norm_gain * grad_normed
        grad_hidden = (inverse * scaled - hidden * inverse ** 3 * lax.optimization_barrier(jnp.mean(hidden * scaled, axis=-1, keepdims=True))).astype(jnp.bfloat16)
        weight_grad = jnp.dot(attn.T, grad_hidden, preferred_element_type=jnp.float32)
        grad_attn = jnp.dot(grad_hidden, out_proj.T, preferred_element_type=jnp.float32).astype(jnp.bfloat16)
        grad_heads = head_split(grad_attn.astype(jnp.float32))
        delta = lax.optimization_barrier(jnp.sum(grad_heads * head_split(attn.astype(jnp.float32)), axis=-1))

        def backward_block(block_inputs):
            block_keys, block_values, block_start = block_inputs
            scores, visible = block_scores(block_keys, block_start)
            probs = jnp.where(visible, jnp.exp(scores - log_norm.T[..., None]), 0.0)
            probs_low = probs.astype(jnp.bfloat16).astype(jnp.float32)
            value_heads = head_split(block_values.astype(jnp.float32))
            grad_probs = jnp.einsum('ihd,jhd->hij', grad_heads, value_heads)
            grad_scores = (probs * (grad_probs - delta.T[..., None])).astype(jnp.bfloat16).astype(jnp.float32)
            grad_v = jnp.einsum('hij,ihd->jhd', probs_low, grad_heads).reshape(TOK_DEV, channels).astype(jnp.bfloat16)
            grad_k = (jnp.einsum('hij,ihd->jhd', grad_scores, query_heads) * softmax_scale).reshape(TOK_DEV, channels).astype(jnp.bfloat16)
            grad_q = jnp.einsum('hij,jhd->ihd', grad_scores, head_split(block_keys.astype(jnp.float32))).reshape(NL, channels) * softmax_scale
            return (grad_k, grad_v, grad_q)
        grad_k, grad_v, grad_q = lax.map(backward_block, (key_blocks, value_blocks, block_starts))
        outputs = (seq_loss, lax.optimization_barrier(jnp.sum(grad_q, axis=0)).astype(jnp.bfloat16), grad_k.reshape(N_SEQ * TOK_DEV, channels), grad_v.reshape(N_SEQ * TOK_DEV, channels))
        return (carried + weight_grad, outputs)
    start_grad = jnp.zeros((HEADS * HD, D), jnp.float32)
    weight_total, results = lax.scan(one_sequence, start_grad, (hist_keys, hist_values, latent_queries, latent_pos, targets))
    losses, grad_queries, grad_keys, grad_values = results
    proj_update = weight_total * lax.rsqrt(jnp.mean(weight_total * weight_total) + epsilon)
    return (losses, grad_queries, grad_keys, grad_values, proj_update)
```

```python
import functools

import jax
import jax.numpy as jnp
from jax import lax
from jax.experimental import pallas as pl
from jax.experimental.pallas import tpu as pltpu
from jax.sharding import PartitionSpec as P

MESH = pl.DeviceIdType.MESH
BF = jnp.bfloat16
F32 = jnp.float32

D = 2048
HD = 128
HEADS = 8
NL = 64
TOK = 128
HC = 1024
NS = 32
NG = 16
NX = 4
NY = 8
SLABS = 16
EPS = 1e-06
LOSS_FACTOR = 64.0
SCALE = HD ** (-0.5)

RANGE_T = ((1,), (1,))


def dot(a, b, dims=((1,), (0,))):
    return lax.dot_general(a, b, (dims, ((), ())), preferred_element_type=F32)


def iota(shape, dim):
    return lax.broadcasted_iota(jnp.int32, shape, dim)


def column_to_row(col, rows):
    wide = jnp.broadcast_to(col, (rows, 128))
    picked = jnp.where(iota((rows, 128), 0) == iota((rows, 128), 1), wide, 0.0)
    return jnp.sum(picked, axis=0, keepdims=True)


def row_to_column(row, rows):
    wide = jnp.broadcast_to(row, (rows, 128))
    picked = jnp.where(iota((rows, 128), 0) == iota((rows, 128), 1), wide, 0.0)
    return jnp.sum(picked, axis=1, keepdims=True)


def wait_bytes(ref, sem):
    pltpu.make_async_copy(ref, ref, sem).wait()


def kernel(
    k_ref, v_ref, q_ref, pos_ref, tgt_ref, w_ref, gain_row_ref, gain_ref, u_ref,
    loss_ref, gq_ref, gk_ref, gv_ref, gw_ref,
    qsend, qbuf, wbuf, wusend, wubuf, osend, obuf, stsend, stbuf, asend, abuf, lsend, lbuf,
    ysend, ybuf, sssend, ssbuf, dsend, dbuf, gqsend, gqbuf, gsend, gbuf, tsend, tbuf,
    s1send, s1buf, s2send, s2buf,
    flat, flat2, sc, awide, lse_s, tgt_s, own_s, kap_s, st_s,
    ssem, rsem,
):
    g = lax.axis_index("grp")
    d = lax.axis_index("seq")
    y, x = d // NX, d % NX
    slab, par = d // 2, d % 2
    owner = 16 * par + g

    def seq_peer(i):
        return lax.rem(d + i, NS)

    def grp_peer(i):
        return lax.rem(g + i, NG)

    barrier = pltpu.get_barrier_semaphore()

    def greet_seq(i, c):
        pl.semaphore_signal(barrier, inc=1, device_id={"grp": g, "seq": seq_peer(i)}, device_id_type=MESH)
        return c

    def greet_grp(i, c):
        pl.semaphore_signal(barrier, inc=1, device_id={"grp": grp_peer(i), "seq": d}, device_id_type=MESH)
        return c

    def greet_tiles(i, c):
        gs, ds = d % 16, 2 * i + d // 16

        @pl.when(jnp.logical_or(gs != g, ds != d))
        def _():
            pl.semaphore_signal(barrier, inc=1, device_id={"grp": gs, "seq": ds}, device_id_type=MESH)

        return c

    lax.fori_loop(1, NS, greet_seq, 0)
    lax.fori_loop(1, NG, greet_grp, 0)
    lax.fori_loop(0, SLABS, greet_tiles, 0)

    def to_seq(src, dst, n):
        def one(i, c):
            t = seq_peer(i)
            pltpu.make_async_remote_copy(
                src_ref=src(t), dst_ref=dst, send_sem=ssem.at[n], recv_sem=rsem.at[n],
                device_id={"grp": g, "seq": t}, device_id_type=MESH,
            ).start()
            return c

        lax.fori_loop(1, NS, one, 0)

    def to_grp(src, dst, n):
        def one(i, c):
            t = grp_peer(i)
            pltpu.make_async_remote_copy(
                src_ref=src(t), dst_ref=dst, send_sem=ssem.at[n], recv_sem=rsem.at[n],
                device_id={"grp": t, "seq": d}, device_id_type=MESH,
            ).start()
            return c

        lax.fori_loop(1, NG, one, 0)

    q32 = q_ref[...].astype(F32)
    for h in range(HEADS):
        own_s[pl.ds(h, 2, stride=8), :] = q32[:, h * HD : (h + 1) * HD]
    qsend[...] = own_s[...].astype(BF)
    qbuf[d] = own_s[...].astype(BF)
    pos = row_to_column(pos_ref[...].astype(F32), NL)
    places = (d * TOK + iota((NL, TOK), 1)).astype(F32)
    visible = places <= pos
    wg = w_ref[...].astype(F32) * gain_row_ref[...]
    wg_high = wg.astype(BF)
    wg_low = (wg - wg_high.astype(F32)).astype(BF)
    wu_own = (dot(wg_high, u_ref[...]) + dot(wg_low, u_ref[...])).astype(BF)
    wusend[...] = wu_own
    wubuf[d] = wu_own
    wbuf[d] = w_ref[:, pl.ds(pl.multiple_of(slab * 128, 128), 128)]

    tiles_out = jnp.where(owner == d, NG - 1, NG)
    pl.semaphore_wait(barrier, NS - 1 + NG - 1 + tiles_out)

    to_seq(lambda t: qsend, qbuf.at[d], 0)
    to_seq(lambda t: w_ref.at[:, pl.ds(pl.multiple_of((t // 2) * 128, 128), 128)], wbuf.at[d], 1)

    wait_bytes(qbuf.at[pl.ds(0, NS - 1)], rsem.at[0])
    flat[...] = qbuf[...].reshape(NL * HEADS, HD).astype(F32)
    lanes = iota((NL, 128), 1)
    ms = jnp.zeros((NL, 128), F32)
    ls = jnp.zeros((NL, 128), F32)
    for h in range(HEADS):
        cols = slice(h * HD, (h + 1) * HD)
        qh = flat[pl.ds(h, NL, stride=8), :].astype(BF)
        s = dot(qh, k_ref[:, cols], RANGE_T) * SCALE
        sc[h] = s
        m = jnp.max(jnp.where(visible, s, -1e30), axis=-1, keepdims=True)
        p = jnp.where(visible, jnp.exp(s - m), 0.0)
        ms = jnp.where(lanes == h, m, ms)
        ls = jnp.where(lanes == h, jnp.sum(p, axis=-1, keepdims=True), ls)
        flat2[pl.ds(h, NL, stride=8), :] = dot(p.astype(BF), v_ref[:, cols])
    o_all = flat2[...].reshape(NS, 16, HD).astype(BF)
    osend[...] = o_all
    st_s[0] = ms
    st_s[1] = ls
    stsend[:, 0, :] = st_s[0, pl.ds(0, NS, stride=2), :]
    stsend[:, 1, :] = st_s[0, pl.ds(1, NS, stride=2), :]
    stsend[:, 2, :] = st_s[1, pl.ds(0, NS, stride=2), :]
    stsend[:, 3, :] = st_s[1, pl.ds(1, NS, stride=2), :]
    to_seq(lambda t: stsend.at[t], stbuf.at[d], 3)
    to_seq(lambda t: osend.at[t], obuf.at[d], 2)
    to_seq(lambda t: wusend, wubuf.at[d], 4)
    stbuf[d] = stsend[d]
    obuf[d] = osend[d]

    wait_bytes(stbuf.at[pl.ds(0, NS - 1)], rsem.at[3])
    weights = []
    head_lane = iota((1, 128), 1)
    for r in range(2):
        mr = stbuf[:, r, :]
        lr = stbuf[:, 2 + r, :]
        best = jnp.max(mr, axis=0, keepdims=True)
        f = jnp.exp(mr - best)
        denom = jnp.sum(lr * f, axis=0, keepdims=True)
        denom = jnp.where(head_lane < HEADS, denom, 1.0)
        weights.append(jnp.transpose(f / denom)[0:HEADS, :])
        row = jnp.where(head_lane < HEADS, best + jnp.log(denom), tgt_ref[0, r].astype(F32))
        lsend[r : r + 1, :] = row
    wait_bytes(obuf.at[pl.ds(0, NS - 1)], rsem.at[2])
    w8 = jnp.concatenate(weights, axis=0)
    total = jnp.zeros((16, HD), F32)
    for b in range(NS):
        total = total + w8[:, b : b + 1] * obuf[b].astype(F32)
    attn_own = total.astype(BF)
    asend[...] = attn_own
    abuf[d] = attn_own
    lbuf[d] = lsend[...]
    to_seq(lambda t: asend, abuf.at[d], 5)
    to_seq(lambda t: lsend, lbuf.at[d], 6)

    wait_bytes(wbuf.at[pl.ds(0, NS - 1)], rsem.at[1])
    wait_bytes(wubuf.at[pl.ds(0, NS - 1)], rsem.at[4])
    wc = wbuf[...].reshape(HC, 128)
    wu = wubuf[...].reshape(HC, 128)
    wait_bytes(abuf.at[pl.ds(0, NS - 1)], rsem.at[5])
    flat2[...] = abuf[...].reshape(NL * HEADS, HD).astype(F32)
    for h in range(HEADS):
        awide[:, h * HD : (h + 1) * HD] = flat2[pl.ds(h, NL, stride=8), :].astype(BF)
    a = awide[...]
    xs = dot(a, wc)
    ss_row = column_to_row(jnp.sum(xs * xs, axis=-1, keepdims=True), NL)
    sssend[...] = ss_row
    ssbuf[slab] = ss_row

    def near_peers(src, dst, n):
        def one(i, c):
            tx = jnp.where(i % 2 == 0, x, NX - 1 - x)
            t = lax.rem(y + i // 2, NY) * NX + tx
            pltpu.make_async_remote_copy(
                src_ref=src(t), dst_ref=dst, send_sem=ssem.at[n], recv_sem=rsem.at[n],
                device_id={"grp": g, "seq": t}, device_id_type=MESH,
            ).start()
            return c

        lax.fori_loop(1, SLABS, one, 0)

    near_peers(lambda t: sssend, ssbuf.at[slab], 7)
    xb = xs.astype(BF)
    for h in range(HEADS):
        flat2[pl.ds(h, NL, stride=8), :] = dot(xb, wc[h * HD : (h + 1) * HD, :], RANGE_T)
    ysend[...] = flat2[...].reshape(NS, 16, HD).astype(BF)
    near_peers(lambda t: ysend.at[t], ybuf.at[slab], 8)
    ybuf[slab] = ysend[d]
    raw = dot(a, wu)

    wait_bytes(lbuf.at[pl.ds(0, NS - 1)], rsem.at[6])
    for r in range(2):
        lb = lbuf[:, r, :]
        for h in range(HEADS):
            lse_s[h, pl.ds(r, NS, stride=2), :] = jnp.broadcast_to(lb[:, h : h + 1], (NS, 128))
        tgt_s[pl.ds(r, NS, stride=2), :] = jnp.broadcast_to(lb[:, HEADS : HEADS + 1], (NS, 128))
    onehot = (lanes.astype(F32) == tgt_s[...]).astype(F32)

    wait_bytes(ssbuf.at[pl.ds(0, SLABS - 1)], rsem.at[7])
    square = row_to_column(jnp.sum(ssbuf[:, 0, :], axis=0, keepdims=True), NL)
    inverse = lax.rsqrt(square * (1.0 / D) + EPS)
    logits = raw * inverse
    top = jnp.max(logits, axis=-1, keepdims=True)
    log_total = top + jnp.log(jnp.sum(jnp.exp(logits - top), axis=-1, keepdims=True))
    per_latent = log_total - jnp.sum(logits * onehot, axis=-1, keepdims=True)
    loss_ref[...] = jnp.sum(per_latent, axis=0, keepdims=True)
    dl = (LOSS_FACTOR * (jnp.exp(logits - log_total) - onehot)).astype(BF)
    mean_xg = jnp.sum(dl.astype(F32) * raw, axis=-1, keepdims=True) * (1.0 / D)
    kappa = inverse * inverse * inverse * mean_xg
    kap_s[...] = jnp.broadcast_to(kappa, (NL, 128))

    u_slab = u_ref[pl.ds(pl.multiple_of(slab * 128, 128), 128), :]
    dn = dot(dl, u_slab, RANGE_T)
    dx = (inverse * gain_ref[pl.ds(slab, 1), :] * dn - kappa * xs).astype(BF)
    a_half = awide[:, pl.ds(pl.multiple_of(par * 512, 512), 512)]
    gpart = dot(a_half, dx, ((0,), (0,)))
    gsend[...] = gpart.reshape(NG, 32, 128).astype(BF)
    to_grp(lambda t: gsend.at[t], gbuf.at[g], 9)
    gbuf[g] = gsend[g]

    for h in range(HEADS):
        flat2[pl.ds(h, NL, stride=8), :] = dot(dl, wu[h * HD : (h + 1) * HD, :], RANGE_T) * inverse
    wait_bytes(ybuf.at[pl.ds(0, SLABS - 1)], rsem.at[8])
    ysum = jnp.sum(ybuf[...].astype(F32), axis=0)
    k2 = jnp.concatenate(
        [jnp.broadcast_to(kap_s[pl.ds(2 * d + r, 1), :], (HEADS, 128)) for r in range(2)], axis=0
    )
    dattn_own = (flat2[pl.ds(pl.multiple_of(d * 16, 16), 16), :] - k2 * ysum).astype(BF)
    dsend[...] = dattn_own
    dbuf[d] = dattn_own
    to_seq(lambda t: dsend, dbuf.at[d], 10)

    wait_bytes(dbuf.at[pl.ds(0, NS - 1)], rsem.at[10])
    flat2[...] = dbuf[...].reshape(NL * HEADS, HD).astype(F32)
    kept = []
    for h in range(HEADS):
        cols = slice(h * HD, (h + 1) * HD)
        d32 = flat2[pl.ds(h, NL, stride=8), :]
        dh = d32.astype(BF)
        delta = jnp.sum(d32 * awide[:, cols].astype(F32), axis=-1, keepdims=True)
        probs = jnp.where(visible, jnp.exp(sc[h] - lse_s[h]), 0.0)
        dp = dot(dh, v_ref[:, cols], RANGE_T)
        ds = (probs * (dp - delta)).astype(BF)
        kept.append((probs.astype(BF), ds, dh))
    for h in range(HEADS):
        cols = slice(h * HD, (h + 1) * HD)
        flat2[pl.ds(h, NL, stride=8), :] = dot(kept[h][1], k_ref[:, cols]) * SCALE
    gqsend[...] = flat2[...].reshape(NS, 16, HD).astype(BF)
    to_seq(lambda t: gqsend.at[t], gqbuf.at[d], 11)
    gqbuf[d] = gqsend[d]

    wait_bytes(gbuf.at[pl.ds(0, NG - 1)], rsem.at[9])
    tile = jnp.sum(gbuf[...].astype(F32), axis=0)
    squares = jnp.sum(jnp.sum(tile * tile, axis=0, keepdims=True), axis=1, keepdims=True)
    s1 = jnp.broadcast_to(squares, (1, 128))
    s1send[...] = s1
    s1buf[d] = s1
    to_seq(lambda t: s1send, s1buf.at[d], 12)
    tsend[...] = tile.astype(BF)

    def one_owner(i, c):
        @pl.when(jnp.logical_or(i > 0, owner != d))
        def _():
            pltpu.make_async_remote_copy(
                src_ref=tsend, dst_ref=tbuf.at[slab], send_sem=ssem.at[13], recv_sem=rsem.at[13],
                device_id={"grp": grp_peer(i), "seq": owner}, device_id_type=MESH,
            ).start()

        return c

    lax.fori_loop(0, NG, one_owner, 0)

    @pl.when(owner == d)
    def _():
        tbuf[slab] = tsend[...]

    for h in range(HEADS):
        cols = slice(h * HD, (h + 1) * HD)
        pr, ds, dh = kept[h]
        gv_ref[:, cols] = dot(pr, dh, ((0,), (0,))).astype(BF)
        qh = flat[pl.ds(h, NL, stride=8), :].astype(BF)
        gk_ref[:, cols] = (dot(ds, qh, ((0,), (0,))) * SCALE).astype(BF)

    wait_bytes(s1buf.at[pl.ds(0, NS - 1)], rsem.at[12])
    s2 = jnp.sum(s1buf[:, 0, :], axis=0, keepdims=True)
    s2send[...] = s2
    s2buf[g] = s2
    to_grp(lambda t: s2send, s2buf.at[g], 14)

    wait_bytes(gqbuf.at[pl.ds(0, NS - 1)], rsem.at[11])
    own_s[...] = jnp.sum(gqbuf[...].astype(F32), axis=0)
    for h in range(HEADS):
        gq_ref[:, h * HD : (h + 1) * HD] = own_s[pl.ds(h, 2, stride=8), :].astype(BF)

    @pl.when(owner == d)
    def _():
        wait_bytes(tbuf.at[pl.ds(0, SLABS - 1)], rsem.at[13])
        wait_bytes(tbuf.at[pl.ds(0, NG - 1)], ssem.at[13])

    @pl.when(owner != d)
    def _():
        wait_bytes(tbuf, rsem.at[13])
        wait_bytes(tbuf, ssem.at[13])

    wait_bytes(s2buf.at[pl.ds(0, NG - 1)], rsem.at[14])
    total_squares = jnp.sum(s2buf[:, 0, :], axis=0, keepdims=True)
    factor = lax.rsqrt(total_squares * (1.0 / (HC * D)) + EPS)
    for j in range(SLABS):
        gw_ref[:, j * 128 : (j + 1) * 128] = tbuf[j].astype(F32) * factor

    for n, ref, count in (
        (0, qbuf, NS - 1), (1, wbuf, NS - 1), (2, obuf, NS - 1), (3, stbuf, NS - 1), (4, wubuf, NS - 1),
        (5, abuf, NS - 1), (6, lbuf, NS - 1), (7, ssbuf, SLABS - 1), (8, ybuf, SLABS - 1), (9, gbuf, NG - 1),
        (10, dbuf, NS - 1), (11, gqbuf, NS - 1), (12, s1buf, NS - 1), (14, s2buf, NG - 1),
    ):
        wait_bytes(ref.at[pl.ds(0, count)], ssem.at[n])


def body(hist_keys, hist_values, latent_queries, latent_pos, targets, out_proj, norm_gain, unembed):
    vmem = pl.BlockSpec(memory_space=pltpu.VMEM)
    smem = pl.BlockSpec(memory_space=pltpu.SMEM)
    pos = jnp.pad(latent_pos, ((0, 0), (0, 128 - NL)))
    rows16 = lambda n: pltpu.VMEM((n, 16, 128), BF)
    rows32 = lambda n: pltpu.VMEM((n, 32, 128), BF)
    loss, gq, gk, gv, gw = pl.pallas_call(
        kernel,
        out_shape=(
            jax.ShapeDtypeStruct((1, 1), F32),
            jax.ShapeDtypeStruct((2, HC), BF),
            jax.ShapeDtypeStruct((TOK, HC), BF),
            jax.ShapeDtypeStruct((TOK, HC), BF),
            jax.ShapeDtypeStruct((32, D), F32),
        ),
        in_specs=[vmem, vmem, vmem, vmem, smem, vmem, vmem, vmem, vmem],
        out_specs=(vmem,) * 5,
        scratch_shapes=[
            pltpu.VMEM((16, 128), BF), rows16(NS),
            rows32(NS), pltpu.VMEM((32, 128), BF), rows32(NS),
            rows16(NS), rows16(NS),
            pltpu.VMEM((NS, 4, 128), F32), pltpu.VMEM((NS, 4, 128), F32),
            pltpu.VMEM((16, 128), BF), rows16(NS),
            pltpu.VMEM((2, 128), F32), pltpu.VMEM((NS, 2, 128), F32),
            rows16(NS), rows16(SLABS),
            pltpu.VMEM((1, 128), F32), pltpu.VMEM((SLABS, 1, 128), F32),
            pltpu.VMEM((16, 128), BF), rows16(NS),
            rows16(NS), rows16(NS),
            rows32(NG), rows32(NG),
            pltpu.VMEM((32, 128), BF), rows32(SLABS),
            pltpu.VMEM((1, 128), F32), pltpu.VMEM((NS, 1, 128), F32),
            pltpu.VMEM((1, 128), F32), pltpu.VMEM((NG, 1, 128), F32),
            pltpu.VMEM((NL * HEADS, 128), F32), pltpu.VMEM((NL * HEADS, 128), F32),
            pltpu.VMEM((HEADS, NL, TOK), F32),
            pltpu.VMEM((NL, HC), BF),
            pltpu.VMEM((HEADS, NL, 128), F32), pltpu.VMEM((NL, 128), F32),
            pltpu.VMEM((16, 128), F32), pltpu.VMEM((NL, 128), F32),
            pltpu.VMEM((2, NL, 128), F32),
            pltpu.SemaphoreType.DMA((15,)), pltpu.SemaphoreType.DMA((15,)),
        ],
        compiler_params=pltpu.CompilerParams(
            collective_id=0, has_side_effects=True, vmem_limit_bytes=32 << 20
        ),
    )(
        hist_keys[0], hist_values[0], latent_queries[0], pos, targets, out_proj,
        norm_gain.reshape(1, D), norm_gain.reshape(SLABS, 128), unembed,
    )
    return loss.reshape(1), gq[None], gk[None], gv[None], gw


def solution(mesh):
    placed = (
        P("grp", "seq", None), P("grp", "seq", None), P("grp", "seq", None), P("grp", None),
        P("grp", "seq"), P("seq", None), P(), P(),
    )
    return jax.shard_map(
        body,
        mesh=mesh,
        in_specs=placed,
        out_specs=(
            P("grp"), P("grp", "seq", None), P("grp", "seq", None), P("grp", "seq", None), P("seq", None),
        ),
        check_vma=False,
    )
```

```python
import functools

import jax
import jax.numpy as jnp
from jax import lax
from jax.experimental import pallas as pl
from jax.experimental.pallas import tpu as pltpu
from jax.sharding import PartitionSpec as P

MESH = pl.DeviceIdType.MESH
BF = jnp.bfloat16
F32 = jnp.float32

D = 2048
HD = 128
HEADS = 8
NL = 64
TOK = 128
HC = 1024
NS = 32
NG = 16
NX = 4
NY = 8
SLABS = 16
EPS = 1e-06
LOSS_FACTOR = 64.0
SCALE = HD ** (-0.5)

RANGE_T = ((1,), (1,))


def dot(a, b, dims=((1,), (0,))):
    return lax.dot_general(a, b, (dims, ((), ())), preferred_element_type=F32)


def iota(shape, dim):
    return lax.broadcasted_iota(jnp.int32, shape, dim)


def column_to_row(col, rows):
    wide = jnp.broadcast_to(col, (rows, 128))
    picked = jnp.where(iota((rows, 128), 0) == iota((rows, 128), 1), wide, 0.0)
    return jnp.sum(picked, axis=0, keepdims=True)


def row_to_column(row, rows):
    wide = jnp.broadcast_to(row, (rows, 128))
    picked = jnp.where(iota((rows, 128), 0) == iota((rows, 128), 1), wide, 0.0)
    return jnp.sum(picked, axis=1, keepdims=True)


def wait_bytes(ref, sem):
    pltpu.make_async_copy(ref, ref, sem).wait()


def kernel(
    k_hbm, v_hbm, q_hbm, pos_hbm, tgt_hbm, w_hbm, gain_row_hbm, gain_hbm, u_hbm,
    loss_ref, gq_ref, gk_hbm, gv_hbm, gw_ref,
    k_ref, v_ref, q_ref, pos_ref, tgt_ref, w_ref, gain_row_ref, gain_ref, u_ref, gk_ref, gv_ref, insem,
    qsend, qbuf, wbuf, wusend, wubuf, osend, obuf, stsend, stbuf, asend, abuf, lsend, lbuf,
    ysend, ybuf, sssend, ssbuf, dsend, dbuf, gqsend, gqbuf, gsend, gbuf, tsend, tbuf, psend, pbuf, gfull,
    s1send, s1buf, s2send, s2buf,
    flat, flat2, sc, awide, lse_s, tgt_s, own_s, kap_s, st_s,
    ssem, rsem,
):
    g = lax.axis_index("grp")
    d = lax.axis_index("seq")
    y, x = d // NX, d % NX
    slab, par = d // 2, d % 2

    def seq_peer(i):
        return lax.rem(d + i, NS)

    def grp_peer(i):
        return lax.rem(g + i, NG)

    barrier = pltpu.get_barrier_semaphore()

    def greet_seq(i, c):
        pl.semaphore_signal(barrier, inc=1, device_id={"grp": g, "seq": seq_peer(i)}, device_id_type=MESH)
        return c

    def greet_grp(i, c):
        pl.semaphore_signal(barrier, inc=1, device_id={"grp": grp_peer(i), "seq": d}, device_id_type=MESH)
        return c

    lax.fori_loop(1, NS, greet_seq, 0)
    lax.fori_loop(1, NG, greet_grp, 0)

    def load(n, src, dst):
        copy = pltpu.make_async_copy(src, dst, insem.at[n])
        copy.start()
        return copy

    q_in = load(0, q_hbm, q_ref)
    pos_in = load(1, pos_hbm, pos_ref)
    k_in = load(2, k_hbm, k_ref)
    v_in = load(3, v_hbm, v_ref)
    w_in = load(4, w_hbm, w_ref)
    u_in = load(5, u_hbm, u_ref)
    row_in = load(6, gain_row_hbm, gain_row_ref)
    gain_in = load(7, gain_hbm, gain_ref)
    tgt_in = load(8, tgt_hbm, tgt_ref)

    def to_seq(src, dst, n):
        def one(i, c):
            t = seq_peer(i)
            pltpu.make_async_remote_copy(
                src_ref=src(t), dst_ref=dst, send_sem=ssem.at[n], recv_sem=rsem.at[n],
                device_id={"grp": g, "seq": t}, device_id_type=MESH,
            ).start()
            return c

        lax.fori_loop(1, NS, one, 0)

    def to_grp(src, dst, n):
        def one(i, c):
            t = grp_peer(i)
            pltpu.make_async_remote_copy(
                src_ref=src(t), dst_ref=dst, send_sem=ssem.at[n], recv_sem=rsem.at[n],
                device_id={"grp": t, "seq": d}, device_id_type=MESH,
            ).start()
            return c

        lax.fori_loop(1, NG, one, 0)

    q_in.wait()
    q32 = q_ref[...].astype(F32)
    for h in range(HEADS):
        own_s[pl.ds(h, 2, stride=8), :] = q32[:, h * HD : (h + 1) * HD]
    qsend[...] = own_s[...].astype(BF)
    qbuf[d] = own_s[...].astype(BF)
    pos_in.wait()
    pos_wide = jnp.broadcast_to(pos_ref[...].astype(F32), (NL, NL))
    pos = jnp.sum(
        jnp.where(iota((NL, NL), 0) == iota((NL, NL), 1), pos_wide, 0.0), axis=1, keepdims=True
    )
    places = (d * TOK + iota((NL, TOK), 1)).astype(F32)
    visible = places <= pos

    pl.semaphore_wait(barrier, NS - 1 + NG - 1)
    to_seq(lambda t: qsend, qbuf.at[d], 0)

    w_in.wait()
    u_in.wait()
    row_in.wait()
    gain_in.wait()
    tgt_in.wait()
    wg = w_ref[...].astype(F32) * gain_row_ref[...]
    wg_high = wg.astype(BF)
    wg_low = (wg - wg_high.astype(F32)).astype(BF)
    wu_own = (dot(wg_high, u_ref[...]) + dot(wg_low, u_ref[...])).astype(BF)
    wusend[...] = wu_own
    wubuf[d] = wu_own
    wbuf[d] = w_ref[:, pl.ds(pl.multiple_of(slab * 128, 128), 128)]
    k_in.wait()
    v_in.wait()

    wait_bytes(qbuf.at[pl.ds(0, NS - 1)], rsem.at[0])
    flat[...] = qbuf[...].reshape(NL * HEADS, HD).astype(F32)
    lanes = iota((NL, 128), 1)
    ms = jnp.zeros((NL, 128), F32)
    ls = jnp.zeros((NL, 128), F32)
    for h in range(HEADS):
        cols = slice(h * HD, (h + 1) * HD)
        qh = flat[pl.ds(h, NL, stride=8), :].astype(BF)
        s = dot(qh, k_ref[:, cols], RANGE_T) * SCALE
        sc[h] = s
        m = jnp.max(jnp.where(visible, s, -1e30), axis=-1, keepdims=True)
        p = jnp.where(visible, jnp.exp(s - m), 0.0)
        ms = jnp.where(lanes == h, m, ms)
        ls = jnp.where(lanes == h, jnp.sum(p, axis=-1, keepdims=True), ls)
        flat2[pl.ds(h, NL, stride=8), :] = dot(p.astype(BF), v_ref[:, cols])
    o_all = flat2[...].reshape(NS, 16, HD).astype(BF)
    osend[...] = o_all
    st_s[0] = ms
    st_s[1] = ls
    stsend[:, 0, :] = st_s[0, pl.ds(0, NS, stride=2), :]
    stsend[:, 1, :] = st_s[0, pl.ds(1, NS, stride=2), :]
    stsend[:, 2, :] = st_s[1, pl.ds(0, NS, stride=2), :]
    stsend[:, 3, :] = st_s[1, pl.ds(1, NS, stride=2), :]
    to_seq(lambda t: stsend.at[t], stbuf.at[d], 3)
    to_seq(lambda t: osend.at[t], obuf.at[d], 2)
    to_seq(lambda t: w_ref.at[:, pl.ds(pl.multiple_of((t // 2) * 128, 128), 128)], wbuf.at[d], 1)
    stbuf[d] = stsend[d]
    obuf[d] = osend[d]

    wait_bytes(stbuf.at[pl.ds(0, NS - 1)], rsem.at[3])
    weights = []
    head_lane = iota((1, 128), 1)
    for r in range(2):
        mr = stbuf[:, r, :]
        lr = stbuf[:, 2 + r, :]
        best = jnp.max(mr, axis=0, keepdims=True)
        f = jnp.exp(mr - best)
        denom = jnp.sum(lr * f, axis=0, keepdims=True)
        denom = jnp.where(head_lane < HEADS, denom, 1.0)
        weights.append(jnp.transpose(f / denom)[0:HEADS, :])
        row = jnp.where(head_lane < HEADS, best + jnp.log(denom), tgt_ref[0:1, r : r + 1].astype(F32))
        lsend[r : r + 1, :] = row
    wait_bytes(obuf.at[pl.ds(0, NS - 1)], rsem.at[2])
    w8 = jnp.concatenate(weights, axis=0)
    total = jnp.zeros((16, HD), F32)
    for b in range(NS):
        total = total + w8[:, b : b + 1] * obuf[b].astype(F32)
    attn_own = total.astype(BF)
    asend[...] = attn_own
    abuf[d] = attn_own
    lbuf[d] = lsend[...]
    to_seq(lambda t: asend, abuf.at[d], 5)
    to_seq(lambda t: lsend, lbuf.at[d], 6)
    to_seq(lambda t: wusend, wubuf.at[d], 4)

    wait_bytes(wbuf.at[pl.ds(0, NS - 1)], rsem.at[1])
    wc = wbuf[...].reshape(HC, 128)
    wait_bytes(abuf.at[pl.ds(0, NS - 1)], rsem.at[5])
    flat2[...] = abuf[...].reshape(NL * HEADS, HD).astype(F32)
    for h in range(HEADS):
        awide[:, h * HD : (h + 1) * HD] = flat2[pl.ds(h, NL, stride=8), :].astype(BF)
    a = awide[...]
    xs = dot(a, wc)
    ss_row = column_to_row(jnp.sum(xs * xs, axis=-1, keepdims=True), NL)
    sssend[...] = ss_row
    ssbuf[slab] = ss_row

    def near_peers(src, dst, n):
        def one(i, c):
            tx = jnp.where(i % 2 == 0, x, NX - 1 - x)
            t = lax.rem(y + i // 2, NY) * NX + tx
            pltpu.make_async_remote_copy(
                src_ref=src(t), dst_ref=dst, send_sem=ssem.at[n], recv_sem=rsem.at[n],
                device_id={"grp": g, "seq": t}, device_id_type=MESH,
            ).start()
            return c

        lax.fori_loop(1, SLABS, one, 0)

    near_peers(lambda t: sssend, ssbuf.at[slab], 7)
    xb = xs.astype(BF)
    for h in range(HEADS):
        flat2[pl.ds(h, NL, stride=8), :] = dot(xb, wc[h * HD : (h + 1) * HD, :], RANGE_T)
    ysend[...] = flat2[...].reshape(NS, 16, HD).astype(BF)
    near_peers(lambda t: ysend.at[t], ybuf.at[slab], 8)
    ybuf[slab] = ysend[d]
    wait_bytes(wubuf.at[pl.ds(0, NS - 1)], rsem.at[4])
    wu = wubuf[...].reshape(HC, 128)
    raw = dot(a, wu)

    wait_bytes(lbuf.at[pl.ds(0, NS - 1)], rsem.at[6])
    for r in range(2):
        lb = lbuf[:, r, :]
        for h in range(HEADS):
            lse_s[h, pl.ds(r, NS, stride=2), :] = jnp.broadcast_to(lb[:, h : h + 1], (NS, 128))
        tgt_s[pl.ds(r, NS, stride=2), :] = jnp.broadcast_to(lb[:, HEADS : HEADS + 1], (NS, 128))
    onehot = (lanes.astype(F32) == tgt_s[...]).astype(F32)

    wait_bytes(ssbuf.at[pl.ds(0, SLABS - 1)], rsem.at[7])
    square = row_to_column(jnp.sum(ssbuf[:, 0, :], axis=0, keepdims=True), NL)
    inverse = lax.rsqrt(square * (1.0 / D) + EPS)
    logits = raw * inverse
    top = jnp.max(logits, axis=-1, keepdims=True)
    log_total = top + jnp.log(jnp.sum(jnp.exp(logits - top), axis=-1, keepdims=True))
    per_latent = log_total - jnp.sum(logits * onehot, axis=-1, keepdims=True)
    loss_ref[...] = jnp.sum(per_latent, axis=0, keepdims=True)
    dl = (LOSS_FACTOR * (jnp.exp(logits - log_total) - onehot)).astype(BF)
    mean_xg = jnp.sum(dl.astype(F32) * raw, axis=-1, keepdims=True) * (1.0 / D)
    kappa = inverse * inverse * inverse * mean_xg
    kap_s[...] = jnp.broadcast_to(kappa, (NL, 128))

    u_slab = u_ref[pl.ds(pl.multiple_of(slab * 128, 128), 128), :]
    dn = dot(dl, u_slab, RANGE_T)
    dx = (inverse * gain_ref[pl.ds(slab, 1), :] * dn - kappa * xs).astype(BF)
    a_half = awide[:, pl.ds(pl.multiple_of(par * 512, 512), 512)]
    gpart = dot(a_half, dx, ((0,), (0,)))
    gfull[...] = gpart
    for i in range(NG):
        for r in range(2):
            gsend[i, r * 16 : (r + 1) * 16, :] = gfull[pl.ds(2 * i + r, 16, stride=32), :].astype(BF)
    to_grp(lambda t: gsend.at[t], gbuf.at[g], 9)
    gbuf[g] = gsend[g]

    for h in range(HEADS):
        flat2[pl.ds(h, NL, stride=8), :] = dot(dl, wu[h * HD : (h + 1) * HD, :], RANGE_T) * inverse
    wait_bytes(ybuf.at[pl.ds(0, SLABS - 1)], rsem.at[8])
    ysum = jnp.sum(ybuf[...].astype(F32), axis=0)
    k2 = jnp.concatenate(
        [jnp.broadcast_to(kap_s[pl.ds(2 * d + r, 1), :], (HEADS, 128)) for r in range(2)], axis=0
    )
    dattn_own = (flat2[pl.ds(pl.multiple_of(d * 16, 16), 16), :] - k2 * ysum).astype(BF)
    dsend[...] = dattn_own
    dbuf[d] = dattn_own
    to_seq(lambda t: dsend, dbuf.at[d], 10)

    wait_bytes(dbuf.at[pl.ds(0, NS - 1)], rsem.at[10])
    flat2[...] = dbuf[...].reshape(NL * HEADS, HD).astype(F32)
    kept = []
    for h in range(HEADS):
        cols = slice(h * HD, (h + 1) * HD)
        d32 = flat2[pl.ds(h, NL, stride=8), :]
        dh = d32.astype(BF)
        delta = jnp.sum(d32 * awide[:, cols].astype(F32), axis=-1, keepdims=True)
        probs = jnp.where(visible, jnp.exp(sc[h] - lse_s[h]), 0.0)
        dp = dot(dh, v_ref[:, cols], RANGE_T)
        ds = (probs * (dp - delta)).astype(BF)
        kept.append((probs.astype(BF), ds, dh))
    for h in range(HEADS):
        cols = slice(h * HD, (h + 1) * HD)
        flat2[pl.ds(h, NL, stride=8), :] = dot(kept[h][1], k_ref[:, cols]) * SCALE
    gqsend[...] = flat2[...].reshape(NS, 16, HD).astype(BF)
    to_seq(lambda t: gqsend.at[t], gqbuf.at[d], 11)
    gqbuf[d] = gqsend[d]

    wait_bytes(gbuf.at[pl.ds(0, NG - 1)], rsem.at[9])
    tile = jnp.sum(gbuf[...].astype(F32), axis=0)
    squares = jnp.sum(jnp.sum(tile * tile, axis=0, keepdims=True), axis=1, keepdims=True)
    s1 = jnp.broadcast_to(squares, (1, 128))
    s1send[...] = s1
    s1buf[d] = s1
    to_seq(lambda t: s1send, s1buf.at[d], 12)
    for r in range(2):
        tsend[:, r, :] = tile[r * 16 : (r + 1) * 16, :]
    half = d // 16
    first = d - 16 * par

    def one_tile(i, c):
        @pl.when(i != first)
        def _():
            pltpu.make_async_remote_copy(
                src_ref=tsend.at[i], dst_ref=tbuf.at[slab], send_sem=ssem.at[13], recv_sem=rsem.at[13],
                device_id={"grp": g, "seq": 16 * par + i}, device_id_type=MESH,
            ).start()

        return c

    lax.fori_loop(0, SLABS, one_tile, 0)

    @pl.when(half == par)
    def _():
        tbuf[slab] = tsend[first]

    for h in range(HEADS):
        cols = slice(h * HD, (h + 1) * HD)
        pr, ds, dh = kept[h]
        gv_ref[:, cols] = dot(pr, dh, ((0,), (0,))).astype(BF)
        qh = flat[pl.ds(h, NL, stride=8), :].astype(BF)
        gk_ref[:, cols] = (dot(ds, qh, ((0,), (0,))) * SCALE).astype(BF)

    gk_out = load(9, gk_ref, gk_hbm)
    gv_out = load(10, gv_ref, gv_hbm)
    wait_bytes(s1buf.at[pl.ds(0, NS - 1)], rsem.at[12])
    s2 = jnp.sum(s1buf[:, 0, :], axis=0, keepdims=True)
    s2send[...] = s2
    s2buf[g] = s2
    to_grp(lambda t: s2send, s2buf.at[g], 14)

    @pl.when(half == par)
    def _():
        wait_bytes(tbuf.at[pl.ds(0, SLABS - 1)], rsem.at[13])
        wait_bytes(tbuf.at[pl.ds(0, SLABS - 1)], ssem.at[13])

    @pl.when(half != par)
    def _():
        wait_bytes(tbuf, rsem.at[13])
        wait_bytes(tbuf, ssem.at[13])

    for r in range(2):
        psend[r * 16 : (r + 1) * 16, :] = tbuf[:, r, :].astype(BF)
    to_grp(lambda t: psend, pbuf.at[g], 15)
    pbuf[g] = psend[...]

    wait_bytes(gqbuf.at[pl.ds(0, NS - 1)], rsem.at[11])
    own_s[...] = jnp.sum(gqbuf[...].astype(F32), axis=0)
    for h in range(HEADS):
        gq_ref[:, h * HD : (h + 1) * HD] = own_s[pl.ds(h, 2, stride=8), :].astype(BF)

    wait_bytes(s2buf.at[pl.ds(0, NG - 1)], rsem.at[14])
    total_squares = jnp.sum(s2buf[:, 0, :], axis=0, keepdims=True)
    factor = lax.rsqrt(total_squares * (1.0 / (HC * D)) + EPS)
    wait_bytes(pbuf.at[pl.ds(0, NG - 1)], rsem.at[15])
    gfull[...] = pbuf[...].reshape(NG * 32, 128).astype(F32)
    for j in range(SLABS):
        gw_ref[:, j * 128 : (j + 1) * 128] = gfull[pl.ds(j, 32, stride=16), :] * factor

    gk_out.wait()
    gv_out.wait()
    for n, ref, count in (
        (0, qbuf, NS - 1), (1, wbuf, NS - 1), (2, obuf, NS - 1), (3, stbuf, NS - 1), (4, wubuf, NS - 1),
        (5, abuf, NS - 1), (6, lbuf, NS - 1), (7, ssbuf, SLABS - 1), (8, ybuf, SLABS - 1), (9, gbuf, NG - 1),
        (10, dbuf, NS - 1), (11, gqbuf, NS - 1), (12, s1buf, NS - 1), (14, s2buf, NG - 1),
        (15, pbuf, NG - 1),
    ):
        wait_bytes(ref.at[pl.ds(0, count)], ssem.at[n])


def write_out(loss, gq, gk, gv, gw, loss_out, gq_out, gk_out, gv_out, gw_out, l_v, q_v, k_v, v_v, w_v, sem_in, sem_out):
    steps = ((gw, w_v, gw_out), (gk, k_v, gk_out), (gv, v_v, gv_out), (gq, q_v, gq_out), (loss, l_v, loss_out))
    arriving = [pltpu.make_async_copy(a, m, sem_in.at[n]) for n, (a, m, b) in enumerate(steps)]
    leaving = [pltpu.make_async_copy(m, b, sem_out.at[n]) for n, (a, m, b) in enumerate(steps)]
    for copy in arriving:
        copy.start()
    for one, other in zip(arriving, leaving):
        one.wait()
        other.start()
    for copy in leaving:
        copy.wait()


def body(hist_keys, hist_values, latent_queries, latent_pos, targets, out_proj, norm_gain, unembed):
    vmem = pl.BlockSpec(memory_space=pltpu.VMEM)
    hbm = pl.BlockSpec(memory_space=pltpu.HBM)
    rows16 = lambda n: pltpu.VMEM((n, 16, 128), BF)
    rows32 = lambda n: pltpu.VMEM((n, 32, 128), BF)
    loss, gq, gk, gv, gw = pl.pallas_call(
        kernel,
        out_shape=(
            jax.ShapeDtypeStruct((1, 1), F32),
            jax.ShapeDtypeStruct((2, HC), BF),
            jax.ShapeDtypeStruct((TOK, HC), BF),
            jax.ShapeDtypeStruct((TOK, HC), BF),
            jax.ShapeDtypeStruct((32, D), F32),
        ),
        in_specs=[hbm] * 9,
        out_specs=(vmem, vmem, hbm, hbm, vmem),
        scratch_shapes=[
            pltpu.VMEM((TOK, HC), BF), pltpu.VMEM((TOK, HC), BF), pltpu.VMEM((2, HC), BF),
            pltpu.VMEM((1, NL), jnp.int32), pltpu.VMEM((1, 2), jnp.int32), pltpu.VMEM((32, D), BF),
            pltpu.VMEM((1, D), F32), pltpu.VMEM((SLABS, 128), F32), pltpu.VMEM((D, 128), BF),
            pltpu.VMEM((TOK, HC), BF), pltpu.VMEM((TOK, HC), BF), pltpu.SemaphoreType.DMA((11,)),
            pltpu.VMEM((16, 128), BF), rows16(NS),
            rows32(NS), pltpu.VMEM((32, 128), BF), rows32(NS),
            rows16(NS), rows16(NS),
            pltpu.VMEM((NS, 4, 128), F32), pltpu.VMEM((NS, 4, 128), F32),
            pltpu.VMEM((16, 128), BF), rows16(NS),
            pltpu.VMEM((2, 128), F32), pltpu.VMEM((NS, 2, 128), F32),
            rows16(NS), rows16(SLABS),
            pltpu.VMEM((1, 128), F32), pltpu.VMEM((SLABS, 1, 128), F32),
            pltpu.VMEM((16, 128), BF), rows16(NS),
            rows16(NS), rows16(NS),
            rows32(NG), rows32(NG),
            pltpu.VMEM((SLABS, 2, 128), F32), pltpu.VMEM((SLABS, 2, 128), F32),
            pltpu.VMEM((32, 128), BF), rows32(NG), pltpu.VMEM((512, 128), F32),
            pltpu.VMEM((1, 128), F32), pltpu.VMEM((NS, 1, 128), F32),
            pltpu.VMEM((1, 128), F32), pltpu.VMEM((NG, 1, 128), F32),
            pltpu.VMEM((NL * HEADS, 128), F32), pltpu.VMEM((NL * HEADS, 128), F32),
            pltpu.VMEM((HEADS, NL, TOK), F32),
            pltpu.VMEM((NL, HC), BF),
            pltpu.VMEM((HEADS, NL, 128), F32), pltpu.VMEM((NL, 128), F32),
            pltpu.VMEM((16, 128), F32), pltpu.VMEM((NL, 128), F32),
            pltpu.VMEM((2, NL, 128), F32),
            pltpu.SemaphoreType.DMA((16,)), pltpu.SemaphoreType.DMA((16,)),
        ],
        compiler_params=pltpu.CompilerParams(
            collective_id=0, has_side_effects=True, vmem_limit_bytes=56 << 20
        ),
    )(
        hist_keys[0], hist_values[0], latent_queries[0], latent_pos, targets, out_proj,
        norm_gain.reshape(1, D), norm_gain.reshape(SLABS, 128), unembed,
    )
    loss, gq, gk, gv, gw = pl.pallas_call(
        write_out,
        out_shape=(
            jax.ShapeDtypeStruct((1, 1), F32),
            jax.ShapeDtypeStruct((2, HC), BF),
            jax.ShapeDtypeStruct((TOK, HC), BF),
            jax.ShapeDtypeStruct((TOK, HC), BF),
            jax.ShapeDtypeStruct((32, D), F32),
        ),
        in_specs=[hbm] * 5,
        out_specs=(hbm,) * 5,
        scratch_shapes=[
            pltpu.VMEM((1, 1), F32), pltpu.VMEM((2, HC), BF), pltpu.VMEM((TOK, HC), BF),
            pltpu.VMEM((TOK, HC), BF), pltpu.VMEM((32, D), F32),
            pltpu.SemaphoreType.DMA((5,)), pltpu.SemaphoreType.DMA((5,)),
        ],
        compiler_params=pltpu.CompilerParams(vmem_limit_bytes=56 << 20),
    )(loss, gq, gk, gv, gw)
    return loss.reshape(1), gq[None], gk[None], gv[None], gw


def solution(mesh):
    placed = (
        P("grp", "seq", None), P("grp", "seq", None), P("grp", "seq", None), P("grp", None),
        P("grp", "seq"), P("seq", None), P(), P(),
    )
    return jax.shard_map(
        body,
        mesh=mesh,
        in_specs=placed,
        out_specs=(
            P("grp"), P("grp", "seq", None), P("grp", "seq", None), P("grp", "seq", None), P("seq", None),
        ),
        check_vma=False,
    )
```

```python
import functools

import jax
import jax.numpy as jnp
from jax import lax
from jax.experimental import pallas as pl
from jax.experimental.pallas import tpu as pltpu
from jax.sharding import PartitionSpec as P

MESH = pl.DeviceIdType.MESH
BF = jnp.bfloat16
F32 = jnp.float32

D = 2048
HD = 128
HEADS = 8
NL = 64
TOK = 128
HC = 1024
NS = 32
NG = 16
NX = 4
NY = 8
SLABS = 16
EPS = 1e-06
LOSS_FACTOR = 64.0
SCALE = HD ** (-0.5)

RANGE_T = ((1,), (1,))


def dot(a, b, dims=((1,), (0,))):
    return lax.dot_general(a, b, (dims, ((), ())), preferred_element_type=F32)


def iota(shape, dim):
    return lax.broadcasted_iota(jnp.int32, shape, dim)


def column_to_row(col, rows):
    wide = jnp.broadcast_to(col, (rows, 128))
    picked = jnp.where(iota((rows, 128), 0) == iota((rows, 128), 1), wide, 0.0)
    return jnp.sum(picked, axis=0, keepdims=True)


def row_to_column(row, rows):
    wide = jnp.broadcast_to(row, (rows, 128))
    picked = jnp.where(iota((rows, 128), 0) == iota((rows, 128), 1), wide, 0.0)
    return jnp.sum(picked, axis=1, keepdims=True)


def wait_bytes(ref, sem):
    pltpu.make_async_copy(ref, ref, sem).wait()


def kernel(
    k_hbm, v_hbm, q_hbm, pos_hbm, tgt_hbm, w_hbm, gain_row_hbm, gain_hbm, u_hbm,
    loss_ref, gq_ref, gk_hbm, gv_hbm, gw_ref,
    k_ref, v_ref, q_ref, pos_ref, tgt_ref, w_ref, gain_row_ref, gain_ref, u_ref, gk_ref, gv_ref, insem,
    qsend, qbuf, wbuf, wusend, wubuf, osend, obuf, stsend, stbuf, asend, abuf, lsend, lbuf,
    ysend, ybuf, sssend, ssbuf, dsend, dbuf, gqsend, gqbuf, gsend, gbuf, tsend, tbuf, psend, pbuf, gfull,
    s1send, s1buf, s2send, s2buf,
    flat, flat2, sc, awide, lse_s, tgt_s, own_s, kap_s, st_s,
    ssem, rsem,
):
    g = lax.axis_index("grp")
    d = lax.axis_index("seq")
    y, x = d // NX, d % NX
    slab, par = d // 2, d % 2

    def spread(i, middle):
        return middle + jnp.where(i % 2 == 0, i // 2, -((i + 1) // 2))

    def seq_peer(i):
        return lax.rem(y + spread(i // NX, NY // 2), NY) * NX + lax.rem(x + spread(i % NX, NX // 2), NX)

    def grp_peer(i):
        return lax.rem(g // 2 + spread(i // 2, 4), NG // 2) * 2 + lax.rem(g + 1 + i, 2)

    barrier = pltpu.get_barrier_semaphore()

    def greet_seq(i, c):
        pl.semaphore_signal(barrier, inc=1, device_id={"grp": g, "seq": seq_peer(i)}, device_id_type=MESH)
        return c

    def greet_grp(i, c):
        pl.semaphore_signal(barrier, inc=1, device_id={"grp": grp_peer(i), "seq": d}, device_id_type=MESH)
        return c

    lax.fori_loop(0, NS - 1, greet_seq, 0)
    lax.fori_loop(0, NG - 1, greet_grp, 0)

    def load(n, src, dst):
        copy = pltpu.make_async_copy(src, dst, insem.at[n])
        copy.start()
        return copy

    q_in = load(0, q_hbm, q_ref)
    pos_in = load(1, pos_hbm, pos_ref)
    k_in = load(2, k_hbm, k_ref)
    v_in = load(3, v_hbm, v_ref)
    w_in = load(4, w_hbm, w_ref)
    u_in = load(5, u_hbm, u_ref)
    row_in = load(6, gain_row_hbm, gain_row_ref)
    gain_in = load(7, gain_hbm, gain_ref)
    tgt_in = load(8, tgt_hbm, tgt_ref)

    def to_seq(*sends):
        def one(i, c):
            t = seq_peer(i)
            for src, dst, n in sends:
                pltpu.make_async_remote_copy(
                    src_ref=src(t), dst_ref=dst, send_sem=ssem.at[n], recv_sem=rsem.at[n],
                    device_id={"grp": g, "seq": t}, device_id_type=MESH,
                ).start()
            return c

        lax.fori_loop(0, NS - 1, one, 0, unroll=True)

    def to_grp(src, dst, n):
        def one(i, c):
            t = grp_peer(i)
            pltpu.make_async_remote_copy(
                src_ref=src(t), dst_ref=dst, send_sem=ssem.at[n], recv_sem=rsem.at[n],
                device_id={"grp": t, "seq": d}, device_id_type=MESH,
            ).start()
            return c

        lax.fori_loop(0, NG - 1, one, 0, unroll=True)

    q_in.wait()
    q32 = q_ref[...].astype(F32)
    for h in range(HEADS):
        own_s[pl.ds(h, 2, stride=8), :] = q32[:, h * HD : (h + 1) * HD]
    qsend[...] = own_s[...].astype(BF)
    qbuf[d] = own_s[...].astype(BF)
    pos_in.wait()
    pos_wide = jnp.broadcast_to(pos_ref[...].astype(F32), (NL, NL))
    pos = jnp.sum(
        jnp.where(iota((NL, NL), 0) == iota((NL, NL), 1), pos_wide, 0.0), axis=1, keepdims=True
    )
    places = (d * TOK + iota((NL, TOK), 1)).astype(F32)
    visible = places <= pos

    w_in.wait()
    u_in.wait()
    row_in.wait()
    gain_in.wait()
    tgt_in.wait()
    wg = w_ref[...].astype(F32) * gain_row_ref[...]
    wg_high = wg.astype(BF)
    wg_low = (wg - wg_high.astype(F32)).astype(BF)
    wu_own = (dot(wg_high, u_ref[...]) + dot(wg_low, u_ref[...])).astype(BF)
    wusend[...] = wu_own
    wubuf[d] = wu_own
    wbuf[d] = w_ref[:, pl.ds(pl.multiple_of(slab * 128, 128), 128)]
    k_in.wait()
    v_in.wait()

    pl.semaphore_wait(barrier, NS - 1 + NG - 1)
    to_seq((lambda t: qsend, qbuf.at[d], 0))
    to_seq((lambda t: w_ref.at[:, pl.ds(pl.multiple_of((t // 2) * 128, 128), 128)], wbuf.at[d], 1))

    wait_bytes(qbuf.at[pl.ds(0, NS - 1)], rsem.at[0])
    flat[...] = qbuf[...].reshape(NL * HEADS, HD).astype(F32)
    lanes = iota((NL, 128), 1)
    ms = jnp.zeros((NL, 128), F32)
    ls = jnp.zeros((NL, 128), F32)
    for h in range(HEADS):
        cols = slice(h * HD, (h + 1) * HD)
        qh = flat[pl.ds(h, NL, stride=8), :].astype(BF)
        s = dot(qh, k_ref[:, cols], RANGE_T) * SCALE
        sc[h] = s
        m = jnp.max(jnp.where(visible, s, -1e30), axis=-1, keepdims=True)
        p = jnp.where(visible, jnp.exp(s - m), 0.0)
        ms = jnp.where(lanes == h, m, ms)
        ls = jnp.where(lanes == h, jnp.sum(p, axis=-1, keepdims=True), ls)
        flat2[pl.ds(h, NL, stride=8), :] = dot(p.astype(BF), v_ref[:, cols])
    o_all = flat2[...].reshape(NS, 16, HD).astype(BF)
    osend[...] = o_all
    st_s[0] = ms
    st_s[1] = ls
    stsend[:, 0, :] = st_s[0, pl.ds(0, NS, stride=2), :]
    stsend[:, 1, :] = st_s[0, pl.ds(1, NS, stride=2), :]
    stsend[:, 2, :] = st_s[1, pl.ds(0, NS, stride=2), :]
    stsend[:, 3, :] = st_s[1, pl.ds(1, NS, stride=2), :]
    to_seq((lambda t: stsend.at[t], stbuf.at[d], 3), (lambda t: osend.at[t], obuf.at[d], 2))
    to_seq((lambda t: wusend, wubuf.at[d], 4))
    stbuf[d] = stsend[d]
    obuf[d] = osend[d]

    wait_bytes(stbuf.at[pl.ds(0, NS - 1)], rsem.at[3])
    weights = []
    head_lane = iota((1, 128), 1)
    for r in range(2):
        mr = stbuf[:, r, :]
        lr = stbuf[:, 2 + r, :]
        best = jnp.max(mr, axis=0, keepdims=True)
        f = jnp.exp(mr - best)
        denom = jnp.sum(lr * f, axis=0, keepdims=True)
        denom = jnp.where(head_lane < HEADS, denom, 1.0)
        weights.append(jnp.transpose(f / denom)[0:HEADS, :])
        row = jnp.where(head_lane < HEADS, best + jnp.log(denom), tgt_ref[0:1, r : r + 1].astype(F32))
        lsend[r : r + 1, :] = row
    wait_bytes(obuf.at[pl.ds(0, NS - 1)], rsem.at[2])
    w8 = jnp.concatenate(weights, axis=0)
    total = jnp.zeros((16, HD), F32)
    for b in range(NS):
        total = total + w8[:, b : b + 1] * obuf[b].astype(F32)
    attn_own = total.astype(BF)
    asend[...] = attn_own
    abuf[d] = attn_own
    lbuf[d] = lsend[...]
    to_seq((lambda t: asend, abuf.at[d], 5), (lambda t: lsend, lbuf.at[d], 6))

    wait_bytes(wbuf.at[pl.ds(0, NS - 1)], rsem.at[1])
    wc = wbuf[...].reshape(HC, 128)
    wait_bytes(abuf.at[pl.ds(0, NS - 1)], rsem.at[5])
    flat2[...] = abuf[...].reshape(NL * HEADS, HD).astype(F32)
    for h in range(HEADS):
        awide[:, h * HD : (h + 1) * HD] = flat2[pl.ds(h, NL, stride=8), :].astype(BF)
    a = awide[...]
    xs = dot(a, wc)
    ss_row = column_to_row(jnp.sum(xs * xs, axis=-1, keepdims=True), NL)
    sssend[...] = ss_row
    ssbuf[slab] = ss_row

    def near_peers(src, dst, n):
        def one(i, c):
            tx = jnp.where(i % 2 == 0, NX - 1 - x, x)
            t = lax.rem(y + spread(i // 2, NY // 2), NY) * NX + tx
            pltpu.make_async_remote_copy(
                src_ref=src(t), dst_ref=dst, send_sem=ssem.at[n], recv_sem=rsem.at[n],
                device_id={"grp": g, "seq": t}, device_id_type=MESH,
            ).start()
            return c

        lax.fori_loop(0, SLABS - 1, one, 0, unroll=True)

    near_peers(lambda t: sssend, ssbuf.at[slab], 7)
    xb = xs.astype(BF)
    for h in range(HEADS):
        flat2[pl.ds(h, NL, stride=8), :] = dot(xb, wc[h * HD : (h + 1) * HD, :], RANGE_T)
    ysend[...] = flat2[...].reshape(NS, 16, HD).astype(BF)
    near_peers(lambda t: ysend.at[t], ybuf.at[slab], 8)
    ybuf[slab] = ysend[d]
    wait_bytes(wubuf.at[pl.ds(0, NS - 1)], rsem.at[4])
    wu = wubuf[...].reshape(HC, 128)
    raw = dot(a, wu)

    wait_bytes(lbuf.at[pl.ds(0, NS - 1)], rsem.at[6])
    for r in range(2):
        lb = lbuf[:, r, :]
        for h in range(HEADS):
            lse_s[h, pl.ds(r, NS, stride=2), :] = jnp.broadcast_to(lb[:, h : h + 1], (NS, 128))
        tgt_s[pl.ds(r, NS, stride=2), :] = jnp.broadcast_to(lb[:, HEADS : HEADS + 1], (NS, 128))
    onehot = (lanes.astype(F32) == tgt_s[...]).astype(F32)

    wait_bytes(ssbuf.at[pl.ds(0, SLABS - 1)], rsem.at[7])
    square = row_to_column(jnp.sum(ssbuf[:, 0, :], axis=0, keepdims=True), NL)
    inverse = lax.rsqrt(square * (1.0 / D) + EPS)
    logits = raw * inverse
    top = jnp.max(logits, axis=-1, keepdims=True)
    log_total = top + jnp.log(jnp.sum(jnp.exp(logits - top), axis=-1, keepdims=True))
    per_latent = log_total - jnp.sum(logits * onehot, axis=-1, keepdims=True)
    loss_ref[...] = jnp.sum(per_latent, axis=0, keepdims=True)
    dl = (LOSS_FACTOR * (jnp.exp(logits - log_total) - onehot)).astype(BF)
    mean_xg = jnp.sum(dl.astype(F32) * raw, axis=-1, keepdims=True) * (1.0 / D)
    kappa = inverse * inverse * inverse * mean_xg
    kap_s[...] = jnp.broadcast_to(kappa, (NL, 128))

    u_slab = u_ref[pl.ds(pl.multiple_of(slab * 128, 128), 128), :]
    dn = dot(dl, u_slab, RANGE_T)
    dx = (inverse * gain_ref[pl.ds(slab, 1), :] * dn - kappa * xs).astype(BF)
    a_half = awide[:, pl.ds(pl.multiple_of(par * 512, 512), 512)]
    gpart = dot(a_half, dx, ((0,), (0,)))
    gfull[...] = gpart
    for i in range(NG):
        for r in range(2):
            gsend[i, r * 16 : (r + 1) * 16, :] = gfull[pl.ds(2 * i + r, 16, stride=32), :].astype(BF)
    to_grp(lambda t: gsend.at[t], gbuf.at[g], 9)
    gbuf[g] = gsend[g]

    for h in range(HEADS):
        flat2[pl.ds(h, NL, stride=8), :] = dot(dl, wu[h * HD : (h + 1) * HD, :], RANGE_T) * inverse
    wait_bytes(ybuf.at[pl.ds(0, SLABS - 1)], rsem.at[8])
    ysum = jnp.sum(ybuf[...].astype(F32), axis=0)
    k2 = jnp.concatenate(
        [jnp.broadcast_to(kap_s[pl.ds(2 * d + r, 1), :], (HEADS, 128)) for r in range(2)], axis=0
    )
    dattn_own = (flat2[pl.ds(pl.multiple_of(d * 16, 16), 16), :] - k2 * ysum).astype(BF)
    dsend[...] = dattn_own
    dbuf[d] = dattn_own
    to_seq((lambda t: dsend, dbuf.at[d], 10))

    wait_bytes(dbuf.at[pl.ds(0, NS - 1)], rsem.at[10])
    flat2[...] = dbuf[...].reshape(NL * HEADS, HD).astype(F32)
    kept = []
    for h in range(HEADS):
        cols = slice(h * HD, (h + 1) * HD)
        d32 = flat2[pl.ds(h, NL, stride=8), :]
        dh = d32.astype(BF)
        delta = jnp.sum(d32 * awide[:, cols].astype(F32), axis=-1, keepdims=True)
        probs = jnp.where(visible, jnp.exp(sc[h] - lse_s[h]), 0.0)
        dp = dot(dh, v_ref[:, cols], RANGE_T)
        ds = (probs * (dp - delta)).astype(BF)
        kept.append((probs.astype(BF), ds, dh))
    for h in range(HEADS):
        cols = slice(h * HD, (h + 1) * HD)
        flat2[pl.ds(h, NL, stride=8), :] = dot(kept[h][1], k_ref[:, cols]) * SCALE
    gqsend[...] = flat2[...].reshape(NS, 16, HD).astype(BF)
    to_seq((lambda t: gqsend.at[t], gqbuf.at[d], 11))
    gqbuf[d] = gqsend[d]

    wait_bytes(gbuf.at[pl.ds(0, NG - 1)], rsem.at[9])
    tile = jnp.sum(gbuf[...].astype(F32), axis=0)
    squares = jnp.sum(jnp.sum(tile * tile, axis=0, keepdims=True), axis=1, keepdims=True)
    s1 = jnp.broadcast_to(squares, (1, 128))
    s1send[...] = s1
    s1buf[d] = s1
    to_seq((lambda t: s1send, s1buf.at[d], 12))
    for r in range(2):
        tsend[:, r, :] = tile[r * 16 : (r + 1) * 16, :]
    half = d // 16
    first = d - 16 * par

    def one_tile(i, c):
        @pl.when(i != first)
        def _():
            pltpu.make_async_remote_copy(
                src_ref=tsend.at[i], dst_ref=tbuf.at[slab], send_sem=ssem.at[13], recv_sem=rsem.at[13],
                device_id={"grp": g, "seq": 16 * par + i}, device_id_type=MESH,
            ).start()

        return c

    lax.fori_loop(0, SLABS, one_tile, 0)

    @pl.when(half == par)
    def _():
        tbuf[slab] = tsend[first]

    for h in range(HEADS):
        cols = slice(h * HD, (h + 1) * HD)
        pr, ds, dh = kept[h]
        gv_ref[:, cols] = dot(pr, dh, ((0,), (0,))).astype(BF)
        qh = flat[pl.ds(h, NL, stride=8), :].astype(BF)
        gk_ref[:, cols] = (dot(ds, qh, ((0,), (0,))) * SCALE).astype(BF)

    gk_out = load(9, gk_ref, gk_hbm)
    gv_out = load(10, gv_ref, gv_hbm)
    wait_bytes(s1buf.at[pl.ds(0, NS - 1)], rsem.at[12])
    s2 = jnp.sum(s1buf[:, 0, :], axis=0, keepdims=True)
    s2send[...] = s2
    s2buf[g] = s2
    to_grp(lambda t: s2send, s2buf.at[g], 14)

    @pl.when(half == par)
    def _():
        wait_bytes(tbuf.at[pl.ds(0, SLABS - 1)], rsem.at[13])
        wait_bytes(tbuf.at[pl.ds(0, SLABS - 1)], ssem.at[13])

    @pl.when(half != par)
    def _():
        wait_bytes(tbuf, rsem.at[13])
        wait_bytes(tbuf, ssem.at[13])

    for r in range(2):
        psend[r * 16 : (r + 1) * 16, :] = tbuf[:, r, :].astype(BF)
    to_grp(lambda t: psend, pbuf.at[g], 15)
    pbuf[g] = psend[...]

    wait_bytes(gqbuf.at[pl.ds(0, NS - 1)], rsem.at[11])
    own_s[...] = jnp.sum(gqbuf[...].astype(F32), axis=0)
    for h in range(HEADS):
        gq_ref[:, h * HD : (h + 1) * HD] = own_s[pl.ds(h, 2, stride=8), :].astype(BF)

    wait_bytes(s2buf.at[pl.ds(0, NG - 1)], rsem.at[14])
    total_squares = jnp.sum(s2buf[:, 0, :], axis=0, keepdims=True)
    factor = lax.rsqrt(total_squares * (1.0 / (HC * D)) + EPS)
    wait_bytes(pbuf.at[pl.ds(0, NG - 1)], rsem.at[15])
    gfull[...] = pbuf[...].reshape(NG * 32, 128).astype(F32)
    for j in range(SLABS):
        gw_ref[:, j * 128 : (j + 1) * 128] = gfull[pl.ds(j, 32, stride=16), :] * factor

    gk_out.wait()
    gv_out.wait()
    for n, ref, count in (
        (0, qbuf, NS - 1), (1, wbuf, NS - 1), (2, obuf, NS - 1), (3, stbuf, NS - 1), (4, wubuf, NS - 1),
        (5, abuf, NS - 1), (6, lbuf, NS - 1), (7, ssbuf, SLABS - 1), (8, ybuf, SLABS - 1), (9, gbuf, NG - 1),
        (10, dbuf, NS - 1), (11, gqbuf, NS - 1), (12, s1buf, NS - 1), (14, s2buf, NG - 1),
        (15, pbuf, NG - 1),
    ):
        wait_bytes(ref.at[pl.ds(0, count)], ssem.at[n])


def write_out(loss, gq, gk, gv, gw, loss_out, gq_out, gk_out, gv_out, gw_out, l_v, q_v, k_v, v_v, w_v, sem_in, sem_out):
    steps = ((gw, w_v, gw_out), (gk, k_v, gk_out), (gv, v_v, gv_out), (gq, q_v, gq_out), (loss, l_v, loss_out))
    arriving = [pltpu.make_async_copy(a, m, sem_in.at[n]) for n, (a, m, b) in enumerate(steps)]
    leaving = [pltpu.make_async_copy(m, b, sem_out.at[n]) for n, (a, m, b) in enumerate(steps)]
    for copy in arriving:
        copy.start()
    for one, other in zip(arriving, leaving):
        one.wait()
        other.start()
    for copy in leaving:
        copy.wait()


def body(hist_keys, hist_values, latent_queries, latent_pos, targets, out_proj, norm_gain, unembed):
    vmem = pl.BlockSpec(memory_space=pltpu.VMEM)
    hbm = pl.BlockSpec(memory_space=pltpu.HBM)
    rows16 = lambda n: pltpu.VMEM((n, 16, 128), BF)
    rows32 = lambda n: pltpu.VMEM((n, 32, 128), BF)
    loss, gq, gk, gv, gw = pl.pallas_call(
        kernel,
        out_shape=(
            jax.ShapeDtypeStruct((1, 1), F32),
            jax.ShapeDtypeStruct((2, HC), BF),
            jax.ShapeDtypeStruct((TOK, HC), BF),
            jax.ShapeDtypeStruct((TOK, HC), BF),
            jax.ShapeDtypeStruct((32, D), F32),
        ),
        in_specs=[hbm] * 9,
        out_specs=(vmem, vmem, hbm, hbm, vmem),
        scratch_shapes=[
            pltpu.VMEM((TOK, HC), BF), pltpu.VMEM((TOK, HC), BF), pltpu.VMEM((2, HC), BF),
            pltpu.VMEM((1, NL), jnp.int32), pltpu.VMEM((1, 2), jnp.int32), pltpu.VMEM((32, D), BF),
            pltpu.VMEM((1, D), F32), pltpu.VMEM((SLABS, 128), F32), pltpu.VMEM((D, 128), BF),
            pltpu.VMEM((TOK, HC), BF), pltpu.VMEM((TOK, HC), BF), pltpu.SemaphoreType.DMA((11,)),
            pltpu.VMEM((16, 128), BF), rows16(NS),
            rows32(NS), pltpu.VMEM((32, 128), BF), rows32(NS),
            rows16(NS), rows16(NS),
            pltpu.VMEM((NS, 4, 128), F32), pltpu.VMEM((NS, 4, 128), F32),
            pltpu.VMEM((16, 128), BF), rows16(NS),
            pltpu.VMEM((2, 128), F32), pltpu.VMEM((NS, 2, 128), F32),
            rows16(NS), rows16(SLABS),
            pltpu.VMEM((1, 128), F32), pltpu.VMEM((SLABS, 1, 128), F32),
            pltpu.VMEM((16, 128), BF), rows16(NS),
            rows16(NS), rows16(NS),
            rows32(NG), rows32(NG),
            pltpu.VMEM((SLABS, 2, 128), F32), pltpu.VMEM((SLABS, 2, 128), F32),
            pltpu.VMEM((32, 128), BF), rows32(NG), pltpu.VMEM((512, 128), F32),
            pltpu.VMEM((1, 128), F32), pltpu.VMEM((NS, 1, 128), F32),
            pltpu.VMEM((1, 128), F32), pltpu.VMEM((NG, 1, 128), F32),
            pltpu.VMEM((NL * HEADS, 128), F32), pltpu.VMEM((NL * HEADS, 128), F32),
            pltpu.VMEM((HEADS, NL, TOK), F32),
            pltpu.VMEM((NL, HC), BF),
            pltpu.VMEM((HEADS, NL, 128), F32), pltpu.VMEM((NL, 128), F32),
            pltpu.VMEM((16, 128), F32), pltpu.VMEM((NL, 128), F32),
            pltpu.VMEM((2, NL, 128), F32),
            pltpu.SemaphoreType.DMA((16,)), pltpu.SemaphoreType.DMA((16,)),
        ],
        compiler_params=pltpu.CompilerParams(
            collective_id=0, has_side_effects=True, vmem_limit_bytes=56 << 20
        ),
    )(
        hist_keys[0], hist_values[0], latent_queries[0], latent_pos, targets, out_proj,
        norm_gain.reshape(1, D), norm_gain.reshape(SLABS, 128), unembed,
    )
    loss, gq, gk, gv, gw = pl.pallas_call(
        write_out,
        out_shape=(
            jax.ShapeDtypeStruct((1, 1), F32),
            jax.ShapeDtypeStruct((2, HC), BF),
            jax.ShapeDtypeStruct((TOK, HC), BF),
            jax.ShapeDtypeStruct((TOK, HC), BF),
            jax.ShapeDtypeStruct((32, D), F32),
        ),
        in_specs=[hbm] * 5,
        out_specs=(hbm,) * 5,
        scratch_shapes=[
            pltpu.VMEM((1, 1), F32), pltpu.VMEM((2, HC), BF), pltpu.VMEM((TOK, HC), BF),
            pltpu.VMEM((TOK, HC), BF), pltpu.VMEM((32, D), F32),
            pltpu.SemaphoreType.DMA((5,)), pltpu.SemaphoreType.DMA((5,)),
        ],
        compiler_params=pltpu.CompilerParams(vmem_limit_bytes=56 << 20),
    )(loss, gq, gk, gv, gw)
    return loss.reshape(1), gq[None], gk[None], gv[None], gw


def solution(mesh):
    placed = (
        P("grp", "seq", None), P("grp", "seq", None), P("grp", "seq", None), P("grp", None),
        P("grp", "seq"), P("seq", None), P(), P(),
    )
    return jax.shard_map(
        body,
        mesh=mesh,
        in_specs=placed,
        out_specs=(
            P("grp"), P("grp", "seq", None), P("grp", "seq", None), P("grp", "seq", None), P("seq", None),
        ),
        check_vma=False,
    )
```

```python
import functools

import jax
import jax.numpy as jnp
from jax import lax
from jax.experimental import pallas as pl
from jax.experimental.pallas import tpu as pltpu
from jax.sharding import PartitionSpec as P

MESH = pl.DeviceIdType.MESH
BF = jnp.bfloat16
F32 = jnp.float32

D = 2048
HD = 128
HEADS = 8
NL = 64
TOK = 128
HC = 1024
NS = 32
NG = 16
NX = 4
NY = 8
SLABS = 16
EPS = 1e-06
LOSS_FACTOR = 64.0
SCALE = HD ** (-0.5)

RANGE_T = ((1,), (1,))


def dot(a, b, dims=((1,), (0,))):
    return lax.dot_general(a, b, (dims, ((), ())), preferred_element_type=F32)


def iota(shape, dim):
    return lax.broadcasted_iota(jnp.int32, shape, dim)


def column_to_row(col, rows):
    wide = jnp.broadcast_to(col, (rows, 128))
    picked = jnp.where(iota((rows, 128), 0) == iota((rows, 128), 1), wide, 0.0)
    return jnp.sum(picked, axis=0, keepdims=True)


def row_to_column(row, rows):
    wide = jnp.broadcast_to(row, (rows, 128))
    picked = jnp.where(iota((rows, 128), 0) == iota((rows, 128), 1), wide, 0.0)
    return jnp.sum(picked, axis=1, keepdims=True)


def wait_bytes(ref, sem):
    pltpu.make_async_copy(ref, ref, sem).wait()


def kernel(
    k_hbm, v_hbm, q_hbm, pos_hbm, tgt_hbm, w_hbm, gain_row_hbm, gain_hbm, u_hbm,
    loss_ref, gq_ref, gk_hbm, gv_hbm, gw_ref,
    k_ref, v_ref, q_ref, pos_ref, tgt_ref, w_ref, gain_row_ref, gain_ref, u_ref, gk_ref, gv_ref, insem,
    qsend, qbuf, wbuf, wusend, wubuf, osend, obuf, stsend, stbuf, asend, abuf, lsend, lbuf,
    ysend, ybuf, sssend, ssbuf, dsend, dbuf, gqsend, gqbuf, gsend, gbuf, tsend, tbuf, psend, pbuf, gfull,
    s1send, s1buf, s2send, s2buf,
    flat, flat2, sc, awide, lse_s, tgt_s, own_s, kap_s, st_s,
    ssem, rsem,
):
    g = lax.axis_index("grp")
    d = lax.axis_index("seq")
    y, x = d // NX, d % NX
    slab, par = d // 2, d % 2

    def spread(i, middle):
        return middle + jnp.where(i % 2 == 0, i // 2, -((i + 1) // 2))

    def seq_peer(i):
        return lax.rem(y + spread(i // NX, NY // 2), NY) * NX + lax.rem(x + spread(i % NX, NX // 2), NX)

    def grp_peer(i):
        return lax.rem(g // 2 + spread(i // 2, 4), NG // 2) * 2 + lax.rem(g + 1 + i, 2)

    barrier = pltpu.get_barrier_semaphore()

    def greet_seq(i, c):
        pl.semaphore_signal(barrier, inc=1, device_id={"grp": g, "seq": seq_peer(i)}, device_id_type=MESH)
        return c

    def greet_grp(i, c):
        pl.semaphore_signal(barrier, inc=1, device_id={"grp": grp_peer(i), "seq": d}, device_id_type=MESH)
        return c

    lax.fori_loop(0, NS - 1, greet_seq, 0)
    lax.fori_loop(0, NG - 1, greet_grp, 0)

    def load(n, src, dst):
        copy = pltpu.make_async_copy(src, dst, insem.at[n])
        copy.start()
        return copy

    q_in = load(0, q_hbm, q_ref)
    pos_in = load(1, pos_hbm, pos_ref)
    k_in = load(2, k_hbm, k_ref)
    v_in = load(3, v_hbm, v_ref)
    w_in = load(4, w_hbm, w_ref)
    u_in = load(5, u_hbm, u_ref)
    row_in = load(6, gain_row_hbm, gain_row_ref)
    gain_in = load(7, gain_hbm, gain_ref)
    tgt_in = load(8, tgt_hbm, tgt_ref)

    def to_seq(*sends):
        def one(i, c):
            t = seq_peer(i)
            for src, dst, n in sends:
                pltpu.make_async_remote_copy(
                    src_ref=src(t), dst_ref=dst, send_sem=ssem.at[n], recv_sem=rsem.at[n],
                    device_id={"grp": g, "seq": t}, device_id_type=MESH,
                ).start()
            return c

        lax.fori_loop(0, NS - 1, one, 0, unroll=True)

    def to_grp(src, dst, n):
        def one(i, c):
            t = grp_peer(i)
            pltpu.make_async_remote_copy(
                src_ref=src(t), dst_ref=dst, send_sem=ssem.at[n], recv_sem=rsem.at[n],
                device_id={"grp": t, "seq": d}, device_id_type=MESH,
            ).start()
            return c

        lax.fori_loop(0, NG - 1, one, 0, unroll=True)

    q_in.wait()
    q32 = q_ref[...].astype(F32)
    for h in range(HEADS):
        own_s[pl.ds(h, 2, stride=8), :] = q32[:, h * HD : (h + 1) * HD]
    qsend[...] = own_s[...].astype(BF)
    qbuf[d] = own_s[...].astype(BF)
    pos_in.wait()
    pos_wide = jnp.broadcast_to(pos_ref[...].astype(F32), (NL, NL))
    pos = jnp.sum(
        jnp.where(iota((NL, NL), 0) == iota((NL, NL), 1), pos_wide, 0.0), axis=1, keepdims=True
    )
    places = (d * TOK + iota((NL, TOK), 1)).astype(F32)
    visible = places <= pos

    w_in.wait()
    u_in.wait()
    row_in.wait()
    gain_in.wait()
    tgt_in.wait()
    wg = w_ref[...].astype(F32) * gain_row_ref[...]
    wg_high = wg.astype(BF)
    wg_low = (wg - wg_high.astype(F32)).astype(BF)
    wu_own = (dot(wg_high, u_ref[...]) + dot(wg_low, u_ref[...])).astype(BF)
    wusend[...] = wu_own
    wubuf[d] = wu_own
    wbuf[d] = w_ref[:, pl.ds(pl.multiple_of(slab * 128, 128), 128)]
    k_in.wait()
    v_in.wait()

    pl.semaphore_wait(barrier, NS - 1 + NG - 1)
    to_seq((lambda t: qsend, qbuf.at[d], 0))
    to_seq((lambda t: w_ref.at[:, pl.ds(pl.multiple_of((t // 2) * 128, 128), 128)], wbuf.at[d], 1))

    wait_bytes(qbuf.at[pl.ds(0, NS - 1)], rsem.at[0])
    flat[...] = qbuf[...].reshape(NL * HEADS, HD).astype(F32)
    lanes = iota((NL, 128), 1)
    ms = jnp.zeros((NL, 128), F32)
    ls = jnp.zeros((NL, 128), F32)
    for h in range(HEADS):
        cols = slice(h * HD, (h + 1) * HD)
        qh = flat[pl.ds(h, NL, stride=8), :].astype(BF)
        s = dot(qh, k_ref[:, cols], RANGE_T) * SCALE
        sc[h] = s
        m = jnp.max(jnp.where(visible, s, -1e30), axis=-1, keepdims=True)
        p = jnp.where(visible, jnp.exp(s - m), 0.0)
        ms = jnp.where(lanes == h, m, ms)
        ls = jnp.where(lanes == h, jnp.sum(p, axis=-1, keepdims=True), ls)
        flat2[pl.ds(h, NL, stride=8), :] = dot(p.astype(BF), v_ref[:, cols])
    o_all = flat2[...].reshape(NS, 16, HD).astype(BF)
    osend[...] = o_all
    st_s[0] = ms
    st_s[1] = ls
    stsend[:, 0, :] = st_s[0, pl.ds(0, NS, stride=2), :]
    stsend[:, 1, :] = st_s[0, pl.ds(1, NS, stride=2), :]
    stsend[:, 2, :] = st_s[1, pl.ds(0, NS, stride=2), :]
    stsend[:, 3, :] = st_s[1, pl.ds(1, NS, stride=2), :]
    to_seq((lambda t: stsend.at[t], stbuf.at[d], 3), (lambda t: osend.at[t], obuf.at[d], 2))
    stbuf[d] = stsend[d]
    obuf[d] = osend[d]

    wait_bytes(stbuf.at[pl.ds(0, NS - 1)], rsem.at[3])
    weights = []
    head_lane = iota((1, 128), 1)
    for r in range(2):
        mr = stbuf[:, r, :]
        lr = stbuf[:, 2 + r, :]
        best = jnp.max(mr, axis=0, keepdims=True)
        f = jnp.exp(mr - best)
        denom = jnp.sum(lr * f, axis=0, keepdims=True)
        denom = jnp.where(head_lane < HEADS, denom, 1.0)
        weights.append(jnp.transpose(f / denom)[0:HEADS, :])
        row = jnp.where(head_lane < HEADS, best + jnp.log(denom), tgt_ref[0:1, r : r + 1].astype(F32))
        lsend[r : r + 1, :] = row
    wait_bytes(obuf.at[pl.ds(0, NS - 1)], rsem.at[2])
    w8 = jnp.concatenate(weights, axis=0)
    total = jnp.zeros((16, HD), F32)
    for b in range(NS):
        total = total + w8[:, b : b + 1] * obuf[b].astype(F32)
    attn_own = total.astype(BF)
    asend[...] = attn_own
    abuf[d] = attn_own
    lbuf[d] = lsend[...]
    to_seq((lambda t: asend, abuf.at[d], 5), (lambda t: lsend, lbuf.at[d], 6))
    to_seq((lambda t: wusend, wubuf.at[d], 4))

    wait_bytes(wbuf.at[pl.ds(0, NS - 1)], rsem.at[1])
    wc = wbuf[...].reshape(HC, 128)
    wait_bytes(abuf.at[pl.ds(0, NS - 1)], rsem.at[5])
    flat2[...] = abuf[...].reshape(NL * HEADS, HD).astype(F32)
    for h in range(HEADS):
        awide[:, h * HD : (h + 1) * HD] = flat2[pl.ds(h, NL, stride=8), :].astype(BF)
    a = awide[...]
    xs = dot(a, wc)
    ss_row = column_to_row(jnp.sum(xs * xs, axis=-1, keepdims=True), NL)
    sssend[...] = ss_row
    ssbuf[slab] = ss_row

    def near_peers(src, dst, n):
        def one(i, c):
            tx = jnp.where(i % 2 == 0, NX - 1 - x, x)
            t = lax.rem(y + spread(i // 2, NY // 2), NY) * NX + tx
            pltpu.make_async_remote_copy(
                src_ref=src(t), dst_ref=dst, send_sem=ssem.at[n], recv_sem=rsem.at[n],
                device_id={"grp": g, "seq": t}, device_id_type=MESH,
            ).start()
            return c

        lax.fori_loop(0, SLABS - 1, one, 0, unroll=True)

    near_peers(lambda t: sssend, ssbuf.at[slab], 7)
    xb = xs.astype(BF)
    for h in range(HEADS):
        flat2[pl.ds(h, NL, stride=8), :] = dot(xb, wc[h * HD : (h + 1) * HD, :], RANGE_T)
    ysend[...] = flat2[...].reshape(NS, 16, HD).astype(BF)
    near_peers(lambda t: ysend.at[t], ybuf.at[slab], 8)
    ybuf[slab] = ysend[d]
    wait_bytes(wubuf.at[pl.ds(0, NS - 1)], rsem.at[4])
    wu = wubuf[...].reshape(HC, 128)
    raw = dot(a, wu)

    wait_bytes(lbuf.at[pl.ds(0, NS - 1)], rsem.at[6])
    for r in range(2):
        lb = lbuf[:, r, :]
        for h in range(HEADS):
            lse_s[h, pl.ds(r, NS, stride=2), :] = jnp.broadcast_to(lb[:, h : h + 1], (NS, 128))
        tgt_s[pl.ds(r, NS, stride=2), :] = jnp.broadcast_to(lb[:, HEADS : HEADS + 1], (NS, 128))
    onehot = (lanes.astype(F32) == tgt_s[...]).astype(F32)

    wait_bytes(ssbuf.at[pl.ds(0, SLABS - 1)], rsem.at[7])
    square = row_to_column(jnp.sum(ssbuf[:, 0, :], axis=0, keepdims=True), NL)
    inverse = lax.rsqrt(square * (1.0 / D) + EPS)
    logits = raw * inverse
    top = jnp.max(logits, axis=-1, keepdims=True)
    log_total = top + jnp.log(jnp.sum(jnp.exp(logits - top), axis=-1, keepdims=True))
    per_latent = log_total - jnp.sum(logits * onehot, axis=-1, keepdims=True)
    loss_ref[...] = jnp.sum(per_latent, axis=0, keepdims=True)
    dl = (LOSS_FACTOR * (jnp.exp(logits - log_total) - onehot)).astype(BF)
    mean_xg = jnp.sum(dl.astype(F32) * raw, axis=-1, keepdims=True) * (1.0 / D)
    kappa = inverse * inverse * inverse * mean_xg
    kap_s[...] = jnp.broadcast_to(kappa, (NL, 128))

    u_slab = u_ref[pl.ds(pl.multiple_of(slab * 128, 128), 128), :]
    dn = dot(dl, u_slab, RANGE_T)
    dx = (inverse * gain_ref[pl.ds(slab, 1), :] * dn - kappa * xs).astype(BF)
    a_half = awide[:, pl.ds(pl.multiple_of(par * 512, 512), 512)]
    gpart = dot(a_half, dx, ((0,), (0,)))
    gfull[...] = gpart
    for i in range(NG):
        for r in range(2):
            gsend[i, r * 16 : (r + 1) * 16, :] = gfull[pl.ds(2 * i + r, 16, stride=32), :].astype(BF)
    to_grp(lambda t: gsend.at[t], gbuf.at[g], 9)
    gbuf[g] = gsend[g]

    for h in range(HEADS):
        flat2[pl.ds(h, NL, stride=8), :] = dot(dl, wu[h * HD : (h + 1) * HD, :], RANGE_T) * inverse
    wait_bytes(ybuf.at[pl.ds(0, SLABS - 1)], rsem.at[8])
    ysum = jnp.sum(ybuf[...].astype(F32), axis=0)
    k2 = jnp.concatenate(
        [jnp.broadcast_to(kap_s[pl.ds(2 * d + r, 1), :], (HEADS, 128)) for r in range(2)], axis=0
    )
    dattn_own = (flat2[pl.ds(pl.multiple_of(d * 16, 16), 16), :] - k2 * ysum).astype(BF)
    dsend[...] = dattn_own
    dbuf[d] = dattn_own
    to_seq((lambda t: dsend, dbuf.at[d], 10))

    wait_bytes(gbuf.at[pl.ds(0, NG - 1)], rsem.at[9])
    tile = jnp.sum(gbuf[...].astype(F32), axis=0)
    squares = jnp.sum(jnp.sum(tile * tile, axis=0, keepdims=True), axis=1, keepdims=True)
    s1 = jnp.broadcast_to(squares, (1, 128))
    s1send[...] = s1
    s1buf[d] = s1
    to_seq((lambda t: s1send, s1buf.at[d], 12))
    for r in range(2):
        tsend[:, r, :] = tile[r * 16 : (r + 1) * 16, :]
    half = d // 16
    first = d - 16 * par

    def one_tile(i, c):
        @pl.when(i != first)
        def _():
            pltpu.make_async_remote_copy(
                src_ref=tsend.at[i], dst_ref=tbuf.at[slab], send_sem=ssem.at[13], recv_sem=rsem.at[13],
                device_id={"grp": g, "seq": 16 * par + i}, device_id_type=MESH,
            ).start()

        return c

    lax.fori_loop(0, SLABS, one_tile, 0)

    @pl.when(half == par)
    def _():
        tbuf[slab] = tsend[first]

    wait_bytes(dbuf.at[pl.ds(0, NS - 1)], rsem.at[10])
    flat2[...] = dbuf[...].reshape(NL * HEADS, HD).astype(F32)
    kept = []
    for h in range(HEADS):
        cols = slice(h * HD, (h + 1) * HD)
        d32 = flat2[pl.ds(h, NL, stride=8), :]
        dh = d32.astype(BF)
        delta = jnp.sum(d32 * awide[:, cols].astype(F32), axis=-1, keepdims=True)
        probs = jnp.where(visible, jnp.exp(sc[h] - lse_s[h]), 0.0)
        dp = dot(dh, v_ref[:, cols], RANGE_T)
        ds = (probs * (dp - delta)).astype(BF)
        kept.append((probs.astype(BF), ds, dh))
    for h in range(HEADS):
        cols = slice(h * HD, (h + 1) * HD)
        flat2[pl.ds(h, NL, stride=8), :] = dot(kept[h][1], k_ref[:, cols]) * SCALE
    gqsend[...] = flat2[...].reshape(NS, 16, HD).astype(BF)
    to_seq((lambda t: gqsend.at[t], gqbuf.at[d], 11))
    gqbuf[d] = gqsend[d]

    wait_bytes(s1buf.at[pl.ds(0, NS - 1)], rsem.at[12])
    s2 = jnp.sum(s1buf[:, 0, :], axis=0, keepdims=True)
    s2send[...] = s2
    s2buf[g] = s2
    to_grp(lambda t: s2send, s2buf.at[g], 14)

    @pl.when(half == par)
    def _():
        wait_bytes(tbuf.at[pl.ds(0, SLABS - 1)], rsem.at[13])
        wait_bytes(tbuf.at[pl.ds(0, SLABS - 1)], ssem.at[13])

    @pl.when(half != par)
    def _():
        wait_bytes(tbuf, rsem.at[13])
        wait_bytes(tbuf, ssem.at[13])

    for r in range(2):
        psend[r * 16 : (r + 1) * 16, :] = tbuf[:, r, :].astype(BF)
    to_grp(lambda t: psend, pbuf.at[g], 15)
    pbuf[g] = psend[...]

    for h in range(HEADS):
        cols = slice(h * HD, (h + 1) * HD)
        pr, ds, dh = kept[h]
        gv_ref[:, cols] = dot(pr, dh, ((0,), (0,))).astype(BF)
        qh = flat[pl.ds(h, NL, stride=8), :].astype(BF)
        gk_ref[:, cols] = (dot(ds, qh, ((0,), (0,))) * SCALE).astype(BF)

    gk_out = load(9, gk_ref, gk_hbm)
    gv_out = load(10, gv_ref, gv_hbm)

    wait_bytes(gqbuf.at[pl.ds(0, NS - 1)], rsem.at[11])
    own_s[...] = jnp.sum(gqbuf[...].astype(F32), axis=0)
    for h in range(HEADS):
        gq_ref[:, h * HD : (h + 1) * HD] = own_s[pl.ds(h, 2, stride=8), :].astype(BF)

    wait_bytes(s2buf.at[pl.ds(0, NG - 1)], rsem.at[14])
    total_squares = jnp.sum(s2buf[:, 0, :], axis=0, keepdims=True)
    factor = lax.rsqrt(total_squares * (1.0 / (HC * D)) + EPS)
    wait_bytes(pbuf.at[pl.ds(0, NG - 1)], rsem.at[15])
    gfull[...] = pbuf[...].reshape(NG * 32, 128).astype(F32)
    for j in range(SLABS):
        gw_ref[:, j * 128 : (j + 1) * 128] = gfull[pl.ds(j, 32, stride=16), :] * factor

    gk_out.wait()
    gv_out.wait()
    for n, ref, count in (
        (0, qbuf, NS - 1), (1, wbuf, NS - 1), (2, obuf, NS - 1), (3, stbuf, NS - 1), (4, wubuf, NS - 1),
        (5, abuf, NS - 1), (6, lbuf, NS - 1), (7, ssbuf, SLABS - 1), (8, ybuf, SLABS - 1), (9, gbuf, NG - 1),
        (10, dbuf, NS - 1), (11, gqbuf, NS - 1), (12, s1buf, NS - 1), (14, s2buf, NG - 1),
        (15, pbuf, NG - 1),
    ):
        wait_bytes(ref.at[pl.ds(0, count)], ssem.at[n])


def write_out(loss, gq, gk, gv, gw, loss_out, gq_out, gk_out, gv_out, gw_out, l_v, q_v, k_v, v_v, w_v, sem_in, sem_out):
    steps = ((gw, w_v, gw_out), (gk, k_v, gk_out), (gv, v_v, gv_out), (gq, q_v, gq_out), (loss, l_v, loss_out))
    arriving = [pltpu.make_async_copy(a, m, sem_in.at[n]) for n, (a, m, b) in enumerate(steps)]
    leaving = [pltpu.make_async_copy(m, b, sem_out.at[n]) for n, (a, m, b) in enumerate(steps)]
    for copy in arriving:
        copy.start()
    for one, other in zip(arriving, leaving):
        one.wait()
        other.start()
    for copy in leaving:
        copy.wait()


def body(hist_keys, hist_values, latent_queries, latent_pos, targets, out_proj, norm_gain, unembed):
    vmem = pl.BlockSpec(memory_space=pltpu.VMEM)
    hbm = pl.BlockSpec(memory_space=pltpu.HBM)
    rows16 = lambda n: pltpu.VMEM((n, 16, 128), BF)
    rows32 = lambda n: pltpu.VMEM((n, 32, 128), BF)
    loss, gq, gk, gv, gw = pl.pallas_call(
        kernel,
        out_shape=(
            jax.ShapeDtypeStruct((1, 1), F32),
            jax.ShapeDtypeStruct((2, HC), BF),
            jax.ShapeDtypeStruct((TOK, HC), BF),
            jax.ShapeDtypeStruct((TOK, HC), BF),
            jax.ShapeDtypeStruct((32, D), F32),
        ),
        in_specs=[hbm] * 9,
        out_specs=(vmem, vmem, hbm, hbm, vmem),
        scratch_shapes=[
            pltpu.VMEM((TOK, HC), BF), pltpu.VMEM((TOK, HC), BF), pltpu.VMEM((2, HC), BF),
            pltpu.VMEM((1, NL), jnp.int32), pltpu.VMEM((1, 2), jnp.int32), pltpu.VMEM((32, D), BF),
            pltpu.VMEM((1, D), F32), pltpu.VMEM((SLABS, 128), F32), pltpu.VMEM((D, 128), BF),
            pltpu.VMEM((TOK, HC), BF), pltpu.VMEM((TOK, HC), BF), pltpu.SemaphoreType.DMA((11,)),
            pltpu.VMEM((16, 128), BF), rows16(NS),
            rows32(NS), pltpu.VMEM((32, 128), BF), rows32(NS),
            rows16(NS), rows16(NS),
            pltpu.VMEM((NS, 4, 128), F32), pltpu.VMEM((NS, 4, 128), F32),
            pltpu.VMEM((16, 128), BF), rows16(NS),
            pltpu.VMEM((2, 128), F32), pltpu.VMEM((NS, 2, 128), F32),
            rows16(NS), rows16(SLABS),
            pltpu.VMEM((1, 128), F32), pltpu.VMEM((SLABS, 1, 128), F32),
            pltpu.VMEM((16, 128), BF), rows16(NS),
            rows16(NS), rows16(NS),
            rows32(NG), rows32(NG),
            pltpu.VMEM((SLABS, 2, 128), F32), pltpu.VMEM((SLABS, 2, 128), F32),
            pltpu.VMEM((32, 128), BF), rows32(NG), pltpu.VMEM((512, 128), F32),
            pltpu.VMEM((1, 128), F32), pltpu.VMEM((NS, 1, 128), F32),
            pltpu.VMEM((1, 128), F32), pltpu.VMEM((NG, 1, 128), F32),
            pltpu.VMEM((NL * HEADS, 128), F32), pltpu.VMEM((NL * HEADS, 128), F32),
            pltpu.VMEM((HEADS, NL, TOK), F32),
            pltpu.VMEM((NL, HC), BF),
            pltpu.VMEM((HEADS, NL, 128), F32), pltpu.VMEM((NL, 128), F32),
            pltpu.VMEM((16, 128), F32), pltpu.VMEM((NL, 128), F32),
            pltpu.VMEM((2, NL, 128), F32),
            pltpu.SemaphoreType.DMA((16,)), pltpu.SemaphoreType.DMA((16,)),
        ],
        compiler_params=pltpu.CompilerParams(
            collective_id=0, has_side_effects=True, vmem_limit_bytes=56 << 20
        ),
    )(
        hist_keys[0], hist_values[0], latent_queries[0], latent_pos, targets, out_proj,
        norm_gain.reshape(1, D), norm_gain.reshape(SLABS, 128), unembed,
    )
    loss, gq, gk, gv, gw = pl.pallas_call(
        write_out,
        out_shape=(
            jax.ShapeDtypeStruct((1, 1), F32),
            jax.ShapeDtypeStruct((2, HC), BF),
            jax.ShapeDtypeStruct((TOK, HC), BF),
            jax.ShapeDtypeStruct((TOK, HC), BF),
            jax.ShapeDtypeStruct((32, D), F32),
        ),
        in_specs=[hbm] * 5,
        out_specs=(hbm,) * 5,
        scratch_shapes=[
            pltpu.VMEM((1, 1), F32), pltpu.VMEM((2, HC), BF), pltpu.VMEM((TOK, HC), BF),
            pltpu.VMEM((TOK, HC), BF), pltpu.VMEM((32, D), F32),
            pltpu.SemaphoreType.DMA((5,)), pltpu.SemaphoreType.DMA((5,)),
        ],
        compiler_params=pltpu.CompilerParams(vmem_limit_bytes=56 << 20),
    )(loss, gq, gk, gv, gw)
    return loss.reshape(1), gq[None], gk[None], gv[None], gw


def solution(mesh):
    placed = (
        P("grp", "seq", None), P("grp", "seq", None), P("grp", "seq", None), P("grp", None),
        P("grp", "seq"), P("seq", None), P(), P(),
    )
    return jax.shard_map(
        body,
        mesh=mesh,
        in_specs=placed,
        out_specs=(
            P("grp"), P("grp", "seq", None), P("grp", "seq", None), P("grp", "seq", None), P("seq", None),
        ),
        check_vma=False,
    )
```
